32 devices in a mesh: groups: 2 (over y), col: 4 (over z), sub: 4 (over x, core).
Axes of the slice: x: 2, y: 2, z: 4, core: 2. Of those that a mesh axis runs over, the one named last changes fastest.
Arguments:
- gcm_state: float32 [2, 72, 32, 512], P(None, None, ('groups', 'col'), 'sub'), parts along dimension 2, may hold values from -6 to 6
- crm_state: bfloat16 [2, 58, 32, 32, 512], P(None, None, None, ('groups', 'col'), 'sub'), parts along dimension 3, may hold values from -6 to 6
- active: int32 [32, 512], P(('groups', 'col'), 'sub'), parts along dimension 0, may hold values from 0 to 1, as said below
- wind_x: float32 [72], replicated, may hold values from 0.5 to 1.5
- wind_y: float32 [72], replicated, may hold values from -1.5 to -0.5
- courant: float32 [58], replicated, may hold values from 0.05 to 0.45
- relax: float32 [2, 58], replicated, may hold values from 0.05 to 0.4
- sat: float32 [58], replicated, may hold values from -4 to 4
- cond_rate: float32 [58], replicated, may hold values from 0.05 to 0.5
Outputs:
- gcm_new: float32 [2, 72, 32, 512], P(None, None, ('groups', 'col'), 'sub'), parts along dimension 2
- crm_new: bfloat16 [2, 58, 32, 32, 512], P(None, None, None, ('groups', 'col'), 'sub'), parts along dimension 3
The draws below stay inside these ranges and needn't reach their ends.
There are 2 independent parts, one for each index of `groups`. The reference program is written for one: setup_inputs(seed, part) draws one part's arguments, and reference() takes and returns one part's arrays. A program takes and returns all parts, laid end to end along the dimension named above; an argument that names none is the same for every part. Nothing has to cross between parts.
Inputs may be any that keep to these rules, and one draw needn't show every extreme that they name: `active`: exactly 2048 entries are 1, and every column of at least one device's block of 4 x 128 columns is 1.
All inputs are finite; a program needn't handle non-finite values.
Results may differ from the reference program's by a relative error of at most 0.001.
The reference program's roundings to bfloat16 on the way (of `mean_change`) count: a program that leaves them out, or rounds other values in their place, can miss the bound.
Values may be sent and summed in bfloat16 or wider, within the bound.
No kernel may reach another device: no remote copies, remote signals or barrier semaphores. Data moves between devices by JAX's collectives and lax.ppermute only.
A program may use at most 64 MiB of HBM per device.

```python
import math
import jax
import jax.numpy as jnp
import numpy as np
from jax import lax

FIELDS = 2
LEV = 72
CLEV = 58
CCOL = 32
SUBSTEPS = 24
NXD = 4
NYD = 128
NX = 16
NY = 512
ACT_DEV = 128
TOTAL_ACT = 2048


def draw_active(key, part):
    key = jax.random.fold_in(key, 11)
    key_heat, key_full, key_base = jax.random.split(key, 3)
    blocks_x = NX // NXD
    blocks_y = NY // NYD
    blocks = blocks_x * blocks_y
    heat = jax.random.randint(key_heat, (blocks,), 0, 64)
    heat = heat * heat
    chosen = jax.random.randint(key_full, (), 0, blocks)
    heat = jnp.where(jnp.arange(blocks) == chosen, 8192, heat)
    region = (jnp.arange(NX) // NXD)[:, None] * blocks_y + (jnp.arange(NY) // NYD)[None, :]
    base = jax.random.randint(key_base, (NX, NY), 0, 4096)
    score = (jnp.take(heat, region) + base).reshape(-1)
    order = jnp.argsort(-score, stable=True)
    flat = jnp.zeros((NX * NY,), jnp.int32).at[order[:TOTAL_ACT]].set(1)
    return flat.reshape(NX, NY)


def block_scale(stream_key, shape, pieces, low, largest):
    factor_of, own = 1.0, jax.random.fold_in(stream_key, 6)
    for position, shards_of in pieces:
        steps = jnp.exp(jax.random.uniform(jax.random.fold_in(own, position), (shards_of,), jnp.float32, low / len(pieces), largest / len(pieces)))
        factor_of = factor_of * jnp.repeat(steps, shape[position] // shards_of).reshape([-1 if axis == position else 1 for axis in range(len(shape))])
    return factor_of


def scatter_about(key, shape, deviation, bound, pieces=(), held_as=jnp.bfloat16):
    values = deviation * jax.random.normal(key, shape, jnp.float32)
    if pieces:
        values = values * block_scale(key, shape, pieces, -0.22, 0.18)
    return jnp.clip(values, -bound, bound).astype(held_as)


def setup_inputs(seed: int = 0, part: int = 0) -> dict:
    arg_keys = jax.random.split(jax.random.key(seed), 10)
    own_keys = jax.random.split(jax.random.fold_in(arg_keys[9], part), 10)
    gcm_state = scatter_about(own_keys[0], (FIELDS, LEV, NX, NY), 1.0, 6.0, ((2, 4), (3, 4)), jnp.float32)
    crm_state = scatter_about(own_keys[1], (FIELDS, CLEV, CCOL, NX, NY), 1.0, 6.0, ((3, 4), (4, 4)))
    active = draw_active(jax.random.fold_in(jax.random.fold_in(arg_keys[9], part), 71), part)
    wind_x = jnp.clip(jax.random.uniform(arg_keys[3], (LEV,), jnp.float32, 0.5, 1.5), 0.5, 1.5)
    wind_y = jnp.clip(jax.random.uniform(arg_keys[4], (LEV,), jnp.float32, -1.5, -0.5), -1.5, -0.5)
    courant = jnp.clip(jax.random.uniform(arg_keys[5], (CLEV,), jnp.float32, 0.05, 0.45), 0.05, 0.45)
    relax = jnp.clip(jnp.exp(jax.random.uniform(arg_keys[6], (FIELDS, CLEV), jnp.float32, math.log(0.05), math.log(0.4))), 0.05, 0.4)
    sat = scatter_about(arg_keys[7], (CLEV,), 1.0, 4.0, (), jnp.float32)
    cond_rate = jnp.clip(jnp.exp(jax.random.uniform(arg_keys[8], (CLEV,), jnp.float32, math.log(0.05), math.log(0.5))), 0.05, 0.5)
    return dict(gcm_state=gcm_state, crm_state=crm_state, active=active, wind_x=wind_x, wind_y=wind_y, courant=courant, relax=relax, sat=sat, cond_rate=cond_rate)


HIGH = lax.Precision.HIGHEST
DT_DYN = 0.05
DT_CLOUD = 0.5
KAPPA = 0.15

def gll_derivative():
    nodes = np.array([-1.0, -1.0 / np.sqrt(5.0), 1.0 / np.sqrt(5.0), 1.0])
    weights = np.array([1.0 / np.prod([nodes[j] - nodes[k] for k in range(4) if k != j]) for j in range(4)])
    deriv = np.zeros((4, 4))
    for i in range(4):
        for j in range(4):
            if i != j:
                deriv[i, j] = weights[j] / weights[i] / (nodes[i] - nodes[j])
        deriv[i, i] = -deriv[i].sum()
    return 2.0 * deriv

def hat_matrix(count_to, count_from):
    dest = (jnp.arange(count_to, dtype=jnp.float32) + 0.5) / count_to
    source = (jnp.arange(count_from, dtype=jnp.float32) + 0.5) / count_from
    hat = jnp.maximum(0.0, 1.0 - jnp.abs(dest[:, None] - source[None, :]) * count_from)
    return hat / lax.optimization_barrier(jnp.sum(hat, axis=1, keepdims=True))

def cloud_model(states, profile, courant, relax, sat, cond_rate):
    slots = states.shape[1]
    fields = relax.shape[0]
    levels = courant.shape[0]
    columns = states.shape[0] // (fields * levels)
    state = states.astype(jnp.float32).reshape(fields, levels, columns, slots)
    prof = profile.astype(jnp.float32).reshape(fields, -1, slots)
    target = jnp.einsum('kl,fls->fks', hat_matrix(levels, prof.shape[1]), prof, precision=HIGH)
    start = state

    def substep(index, current):
        upwind = current - jnp.roll(current, 1, axis=2)
        above = jnp.concatenate([current[:, 1:], current[:, -1:]], axis=1)
        below = jnp.concatenate([current[:, :1], current[:, :-1]], axis=1)
        change = -courant[None, :, None, None] * upwind + KAPPA * (above + below - 2.0 * current) - DT_CLOUD * relax[:, :, None, None] * (current - target[:, :, None, :])
        condense = DT_CLOUD * cond_rate[:, None, None] * jnp.tanh(current[1] - sat[:, None, None])
        return current + change + jnp.stack([condense, -condense])
    state = lax.fori_loop(0, SUBSTEPS, substep, state)
    mean_change = lax.optimization_barrier(jnp.mean(state - start, axis=2)).astype(jnp.bfloat16)
    return (state.astype(jnp.bfloat16).reshape(-1, slots), mean_change.reshape(-1, slots))

def edge_average(field, axis):
    count = field.shape[axis]
    shape = [1] * field.ndim
    shape[axis] = count
    node = (jnp.arange(count) % 4).reshape(shape)
    before = jnp.roll(field, 1, axis=axis)
    after = jnp.roll(field, -1, axis=axis)
    return jnp.where(node == 0, 0.5 * (field + before), jnp.where(node == 3, 0.5 * (field + after), field))

def reference(gcm_state, crm_state, active, wind_x, wind_y, courant, relax, sat, cond_rate):
    fields, levels, size_x, size_y = gcm_state.shape
    cloud_levels = courant.shape[0]
    deriv = jnp.asarray(gll_derivative(), jnp.float32)
    elements = gcm_state.reshape(fields, levels, size_x // 4, 4, size_y // 4, 4)
    along_x = jnp.einsum('ij,flajbc->flaibc', deriv, elements, precision=HIGH).reshape(gcm_state.shape)
    along_y = jnp.einsum('ij,flabcj->flabci', deriv, elements, precision=HIGH).reshape(gcm_state.shape)
    tendency = -(wind_x[None, :, None, None] * along_x + wind_y[None, :, None, None] * along_y)
    shared = edge_average(edge_average(tendency, 2), 3)
    dynamic = gcm_state + DT_DYN * shared
    flat_active = active.reshape(-1)
    picked = jnp.nonzero(flat_active, size=TOTAL_ACT)[0].astype(jnp.int32)
    profiles = gcm_state.reshape(fields * levels, -1).astype(jnp.bfloat16)
    states = crm_state.reshape(-1, size_x * size_y)
    blocks = picked.reshape(-1, ACT_DEV)

    def run(block):
        return cloud_model(jnp.take(states, block, axis=1), jnp.take(profiles, block, axis=1), courant, relax, sat, cond_rate)
    new_states, changes = lax.map(run, blocks)
    new_states = jnp.transpose(new_states, (1, 0, 2)).reshape(states.shape[0], -1)
    changes = jnp.transpose(changes, (1, 0, 2)).reshape(fields, cloud_levels, -1)
    feedback = jnp.einsum('lk,fks->fls', hat_matrix(levels, cloud_levels), changes.astype(jnp.float32), precision=HIGH)
    gcm_flat = dynamic.reshape(fields, levels, -1)
    gcm_flat = gcm_flat.at[:, :, picked].set(gcm_flat[:, :, picked] + feedback)
    crm_flat = states.at[:, picked].set(new_states)
    return (gcm_flat.reshape(gcm_state.shape), crm_flat.reshape(crm_state.shape))
```

```python
import functools

import jax
import jax.numpy as jnp
import numpy as np
from jax import lax
from jax.experimental import pallas as pl
from jax.experimental.pallas import tpu as pltpu
from jax.sharding import PartitionSpec as P

SUBSTEPS = 24
DT_DYN = 0.05
DT_CLOUD = 0.5
KAPPA = 0.15
HIGH = lax.Precision.HIGHEST
BLOCK = 8


def gll_derivative():
    nodes = np.array([-1.0, -1.0 / np.sqrt(5.0), 1.0 / np.sqrt(5.0), 1.0])
    weights = np.array(
        [1.0 / np.prod([nodes[j] - nodes[k] for k in range(4) if k != j]) for j in range(4)]
    )
    deriv = np.zeros((4, 4))
    for i in range(4):
        for j in range(4):
            if i != j:
                deriv[i, j] = weights[j] / weights[i] / (nodes[i] - nodes[j])
        deriv[i, i] = -deriv[i].sum()
    return 2.0 * deriv


def hat_rows(count_to, count_from):
    dest = (np.arange(count_to) + 0.5) / count_to
    source = (np.arange(count_from) + 0.5) / count_from
    hat = np.maximum(0.0, 1.0 - np.abs(dest[:, None] - source[None, :]) * count_from)
    hat = hat / hat.sum(axis=1, keepdims=True)
    return [[(int(c), float(row[c])) for c in np.nonzero(row > 1e-9)[0]] for row in hat]


def lanes_of(shape):
    return lax.broadcasted_iota(jnp.int32, shape, len(shape) - 1)


def rows_of(shape):
    return lax.broadcasted_iota(jnp.int32, shape, len(shape) - 2)


def tendency_kernel(levels, wind_x, wind_y, gcm, tend, first, last, ends):
    deriv = gll_derivative()
    rows, lanes = gcm.shape
    side_a, side_b = rows_of((lanes, lanes)), lanes_of((lanes, lanes))
    step_y = jnp.zeros((lanes, lanes), jnp.float32)
    for m in range(4):
        for n in range(4):
            step_y = jnp.where((side_a % 4 == m) & (side_b % 4 == n), float(deriv[n, m]), step_y)
    step_y = jnp.where(side_a // 4 == side_b // 4, step_y, 0.0)
    tend[...] = jnp.dot(gcm[...], step_y, precision=HIGH, preferred_element_type=jnp.float32)
    row = rows_of((8, lanes))
    low = row < 4
    factors = {}
    for shift in range(-3, 4):
        factor = jnp.zeros((8, lanes), jnp.float32)
        for i in range(4):
            if 0 <= i - shift < 4:
                factor = jnp.where(row % 4 == i, float(deriv[i, i - shift]), factor)
        factors[shift] = factor
    for v in range(rows // 8):
        at = slice(8 * v, 8 * v + 8)
        lev = 2 * v % levels
        here = gcm[at, :]
        along_x = factors[0] * here
        for shift in (-3, -2, -1, 1, 2, 3):
            along_x = along_x + factors[shift] * pltpu.roll(here, shift % 8, 0)
        blow_x = jnp.where(low, wind_x[lev], wind_x[lev + 1])
        blow_y = jnp.where(low, wind_y[lev], wind_y[lev + 1])
        tend[at, :] = -(blow_x * along_x + blow_y * tend[at, :])
    count = rows // 4
    first[...] = tend[pl.ds(0, count, stride=4), :]
    last[...] = tend[pl.ds(3, count, stride=4), :]
    pick = jnp.where(
        lanes_of((8, lanes)) == jnp.where(rows_of((8, lanes)) == 0, 0, lanes - 1), 1.0, 0.0
    )
    edge = lax.dot_general(
        pick, tend[...], (((1,), (1,)), ((), ())), precision=HIGH, preferred_element_type=jnp.float32
    )
    ends[:, :rows] = edge[:2]
    ends[:, rows:] = jnp.zeros((2, ends.shape[1] - rows), jnp.float32)


def dynamic_kernel(levels, cloud_levels, place, gcm, tend, before, after, ends, change, out, work):
    rows, lanes = gcm.shape
    count = rows // 4
    work[...] = tend[...]
    work[pl.ds(0, count, stride=4), :] = before[...]
    work[pl.ds(3, count, stride=4), :] = after[...]
    width = ends.shape[2]
    lane = lanes_of((2, width))

    def side(base):
        mid, low, high = ends[place[base]], ends[place[base + 1]], ends[place[base + 2]]
        other = jnp.where(
            lane % 4 == 0,
            pltpu.roll(low, width - 3, 1),
            jnp.where(lane % 4 == 3, pltpu.roll(high, 3, 1), mid),
        )
        return 0.5 * (mid + other)

    left, right = side(0), side(3)
    pair = jnp.concatenate([left[1:2], right[0:1], jnp.zeros((6, width), jnp.float32)], axis=0)
    row8, lane8 = rows_of((8, lanes)), lanes_of((8, lanes))
    spread = jnp.where((row8 < 2) & (lane8 == jnp.where(row8 == 0, 0, lanes - 1)), 1.0, 0.0)
    halo = lax.dot_general(
        pair, spread, (((0,), (0,)), ((), ())), precision=HIGH, preferred_element_type=jnp.float32
    )
    low = row8 < 4
    hats = hat_rows(levels, cloud_levels)

    def feedback(field, lev):
        total = None
        for k, weight in hats[lev]:
            term = weight * change[field, k]
            total = term if total is None else total + term
        return total

    for v in range(rows // 8):
        at = slice(8 * v, 8 * v + 8)
        field, lev = divmod(2 * v, levels)
        shared_x = 0.5 * (tend[at, :] + work[at, :])
        beside = jnp.where(
            lane8 % 4 == 0,
            pltpu.roll(shared_x, 1, 1),
            jnp.where(lane8 % 4 == 3, pltpu.roll(shared_x, lanes - 1, 1), shared_x),
        )
        beside = jnp.where((lane8 == 0) | (lane8 == lanes - 1), halo[at, :], beside)
        shared = 0.5 * (shared_x + beside)
        dynamic = gcm[at, :] + DT_DYN * shared
        out[at, :] = dynamic + jnp.where(low, feedback(field, lev), feedback(field, lev + 1))


def cloud_kernel(
    courant, relax, sat, cond_rate, gcm, active, crm, new, change,
    held, one, two, fixed, other, begin, profile, in_sem, out_sem,
):
    fields, levels, rows, lanes = crm.shape
    half_tiles = rows // 16
    tiles = rows // 8
    source_levels = profile.shape[1]
    chunk = levels // 2
    low = rows_of((8, lanes)) < 4

    def piece(f, c):
        return pl.ds(c * chunk, chunk)

    loads = [
        pltpu.make_async_copy(
            crm.at[f, pl.ds(c * chunk, chunk)], held.at[f, pl.ds(c * chunk, chunk)], in_sem.at[f, c]
        )
        for f in range(fields)
        for c in range(2)
    ]
    for load in loads:
        load.start()

    for f in range(fields):
        for v in range(source_levels // 2):
            base = (f * source_levels + 2 * v) * 4
            pair = gcm[base : base + 8, :].astype(jnp.bfloat16).astype(jnp.float32)
            swapped = pltpu.roll(pair, 4, 0)
            profile[f, 2 * v] = jnp.where(low, pair, swapped)
            profile[f, 2 * v + 1] = jnp.where(low, swapped, pair)
    for k, entries in enumerate(hat_rows(levels, source_levels)):
        for f in range(fields):
            total = None
            for l, weight in entries:
                term = weight * profile[f, l]
                total = term if total is None else total + term
            fixed[f, k] = total

    def forward(k, carry):
        ends = jnp.where((k == 0) | (k == levels - 1), KAPPA, 2.0 * KAPPA)
        result = []
        for f in range(fields):
            ratio, value = carry[f]
            rate = DT_CLOUD * relax[f, k]
            scale = 1.0 / (jnp.full((8, lanes), ends + rate, jnp.float32) - KAPPA * ratio)
            value = (rate * fixed[f, k] + KAPPA * value) * scale
            ratio = KAPPA * scale
            fixed[f, k] = value
            begin[f, k] = ratio
            result.append((ratio, value))
        return tuple(result)

    zero = jnp.zeros((8, lanes), jnp.float32)
    lax.fori_loop(0, levels, forward, tuple((zero, zero) for _ in range(fields)))

    def backward(i, carry):
        k = levels - 1 - i
        result = []
        for f in range(fields):
            value = fixed[f, k] + begin[f, k] * carry[f]
            fixed[f, k] = value
            result.append(value)
        other[k] = result[1] - sat[k]
        return tuple(result)

    lax.fori_loop(0, levels, backward, tuple(zero for _ in range(fields)))

    def unpack(f):
        def at(k, _):
            block = held[f, k].astype(jnp.float32)
            steady = fixed[f, k]
            total = zero
            for u in range(half_tiles):
                near, far = block[8 * u : 8 * u + 8], block[8 * (u + half_tiles) : 8 * (u + half_tiles) + 8]
                even = jnp.where(low, near, pltpu.roll(far, 4, 0))
                odd = jnp.where(low, pltpu.roll(near, 4, 0), far)
                total = total + (even + odd)
                one[f, k, 16 * u : 16 * u + 8, :] = even - steady
                one[f, k, 16 * u + 8 : 16 * u + 16, :] = odd - steady
            begin[f, k] = total
            return 0

        return at

    for i, load in enumerate(loads):
        load.wait()
        f, c = divmod(i, 2)
        lax.fori_loop(c * chunk, (c + 1) * chunk, unpack(f), 0)

    def advance(src, dst, first, count, scale, inverse):
        ks = [first + i for i in range(count)]
        reach = [jnp.maximum(first - 1, 0)] + ks + [jnp.minimum(first + count, levels - 1)]
        shift = [courant[k] * (1.0 / KAPPA) for k in ks]
        keep = [
            [
                (1.0 - 2.0 * KAPPA - courant[k] - DT_CLOUD * relax[f, k]) * (1.0 / KAPPA)
                for k in ks
            ]
            for f in range(fields)
        ]
        rate = [DT_CLOUD * cond_rate[k] * inverse for k in ks]
        offset = [other[k] for k in ks]
        left = [
            [pltpu.roll(src[f, k, rows - 8 : rows, :], 4, 0) for k in ks] for f in range(fields)
        ]
        for w in range(tiles):
            at = slice(8 * w, 8 * w + 8)
            here = [[src[f, k, at, :] for k in reach] for f in range(fields)]
            for i, k in enumerate(ks):
                condense = rate[i] * jnp.tanh(here[1][i + 1] * scale + offset[i])
                for f in range(fields):
                    moved = (here[f][i] + here[f][i + 2]) + (
                        keep[f][i] * here[f][i + 1] + shift[i] * left[f][i]
                    )
                    dst[f, k, at, :] = moved + condense if f == 0 else moved - condense
            left = [here[f][1:-1] for f in range(fields)]

    def substep(src, dst, scale, inverse):
        whole = levels // BLOCK

        def step(b, _):
            advance(src, dst, b * BLOCK, BLOCK, scale, inverse)
            return 0

        lax.fori_loop(0, whole, step, 0)
        if levels % BLOCK:
            advance(src, dst, whole * BLOCK, levels % BLOCK, scale, inverse)

    def two_substeps(_, carry):
        scale, inverse = carry
        substep(one, two, scale, inverse)
        scale, inverse = scale * KAPPA, inverse * (1.0 / KAPPA)
        substep(two, one, scale, inverse)
        return scale * KAPPA, inverse * (1.0 / KAPPA)

    final, _ = lax.fori_loop(
        0, SUBSTEPS // 2, two_substeps, (jnp.float32(1.0), jnp.float32(1.0 / KAPPA))
    )

    chosen = jnp.concatenate([active[...], active[...]], axis=0) > 0
    share = 2.0 / rows * 2.0

    def pack(f):
        def at(k, _):
            steady = fixed[f, k]
            block = held[f, k].astype(jnp.float32)
            total = zero
            near, far = [], []
            for u in range(half_tiles):
                even = one[f, k, 16 * u : 16 * u + 8, :] * final + steady
                odd = one[f, k, 16 * u + 8 : 16 * u + 16, :] * final + steady
                total = total + (even + odd)
                near.append(jnp.where(low, even, pltpu.roll(odd, 4, 0)))
                far.append(jnp.where(low, pltpu.roll(even, 4, 0), odd))
            tiles_new = [
                jnp.where(chosen, tile, block[8 * u : 8 * u + 8]) for u, tile in enumerate(near + far)
            ]
            held[f, k] = jnp.concatenate(tiles_new, axis=0).astype(jnp.bfloat16)
            total = total - begin[f, k]
            total = (total + pltpu.roll(total, 4, 0)) * share
            total = total.astype(jnp.bfloat16).astype(jnp.float32)
            change[f, k] = jnp.where(chosen, total, 0.0)
            return 0

        return at

    stores = []
    for f in range(fields):
        for c in range(2):
            lax.fori_loop(c * chunk, (c + 1) * chunk, pack(f), 0)
            store = pltpu.make_async_copy(
                held.at[f, pl.ds(c * chunk, chunk)], new.at[f, pl.ds(c * chunk, chunk)], out_sem.at[f, c]
            )
            store.start()
            stores.append(store)
    for store in stores:
        store.wait()


def body(gcm_state, crm_state, active, wind_x, wind_y, courant, relax, sat, cond_rate):
    fields, levels, rows_x, lanes = gcm_state.shape
    cloud_levels, cloud_columns = crm_state.shape[1:3]
    rows = fields * levels * rows_x
    gcm = gcm_state.reshape(rows, lanes)
    crm = crm_state.reshape(fields, cloud_levels, cloud_columns * rows_x, lanes)
    smem = pl.BlockSpec(memory_space=pltpu.SMEM)
    vmem = pl.BlockSpec(memory_space=pltpu.VMEM)
    anywhere = pl.BlockSpec(memory_space=pl.ANY)
    f32 = jnp.float32

    width = (rows + 127) // 128 * 128
    tend, first, last, ends = pl.pallas_call(
        functools.partial(tendency_kernel, levels),
        out_shape=(
            jax.ShapeDtypeStruct((rows, lanes), f32),
            jax.ShapeDtypeStruct((rows // rows_x, lanes), f32),
            jax.ShapeDtypeStruct((rows // rows_x, lanes), f32),
            jax.ShapeDtypeStruct((2, width), f32),
        ),
        in_specs=[smem, smem, vmem],
        out_specs=(vmem, vmem, vmem, vmem),
        name="tendency",
    )(wind_x, wind_y, gcm)

    count_x, count_y = lax.axis_size("col"), lax.axis_size("sub")
    before = lax.ppermute(last, "col", [(i, (i + 1) % count_x) for i in range(count_x)])
    after = lax.ppermute(first, "col", [((i + 1) % count_x, i) for i in range(count_x)])
    all_ends = lax.all_gather(ends, ("col", "sub"), axis=0)
    at_x, at_y = lax.axis_index("col"), lax.axis_index("sub")
    place = jnp.stack(
        [
            (at_x + dx) % count_x * count_y + (at_y + dy) % count_y
            for dy in (-1, 1)
            for dx in (0, -1, 1)
        ]
    ).astype(jnp.int32)

    slots = (fields, cloud_levels, cloud_columns * rows_x, lanes)
    new, change = pl.pallas_call(
        cloud_kernel,
        out_shape=(
            jax.ShapeDtypeStruct(slots, jnp.bfloat16),
            jax.ShapeDtypeStruct((fields, cloud_levels, 8, lanes), f32),
        ),
        in_specs=[smem, smem, smem, smem, vmem, vmem, anywhere],
        out_specs=(anywhere, vmem),
        scratch_shapes=[
            pltpu.VMEM(slots, jnp.bfloat16),
            pltpu.VMEM(slots, f32),
            pltpu.VMEM(slots, f32),
            pltpu.VMEM((fields, cloud_levels, 8, lanes), f32),
            pltpu.VMEM((cloud_levels, 8, lanes), f32),
            pltpu.VMEM((fields, cloud_levels, 8, lanes), f32),
            pltpu.VMEM((fields, levels, 8, lanes), f32),
            pltpu.SemaphoreType.DMA((fields, 2)),
            pltpu.SemaphoreType.DMA((fields, 2)),
        ],
        compiler_params=pltpu.CompilerParams(vmem_limit_bytes=48 << 20),
        cost_estimate=pl.CostEstimate(
            flops=60_000_000, bytes_accessed=200_000_000, transcendentals=20_000_000
        ),
        name="cloud",
    )(courant, relax, sat, cond_rate, gcm, active, crm)

    out = pl.pallas_call(
        functools.partial(dynamic_kernel, levels, cloud_levels),
        out_shape=jax.ShapeDtypeStruct((rows, lanes), f32),
        in_specs=[smem] + [vmem] * 6,
        out_specs=vmem,
        scratch_shapes=[pltpu.VMEM((rows, lanes), f32)],
        name="dynamic",
    )(place, gcm, tend, before, after, all_ends, change)
    return out.reshape(gcm_state.shape), new.reshape(crm_state.shape)


def solution(mesh):
    placed = (
        P(None, None, ("groups", "col"), "sub"),
        P(None, None, None, ("groups", "col"), "sub"),
        P(("groups", "col"), "sub"),
        P(),
        P(),
        P(),
        P(),
        P(),
        P(),
    )
    return jax.shard_map(
        body,
        mesh=mesh,
        in_specs=placed,
        out_specs=(
            P(None, None, ("groups", "col"), "sub"),
            P(None, None, None, ("groups", "col"), "sub"),
        ),
        check_vma=False,
    )
```

```python
import functools

import jax
import jax.numpy as jnp
import numpy as np
from jax import lax
from jax.experimental import pallas as pl
from jax.experimental.pallas import tpu as pltpu
from jax.sharding import PartitionSpec as P

SUBSTEPS = 24
DT_DYN = 0.05
DT_CLOUD = 0.5
KAPPA = 0.15
HIGH = lax.Precision.HIGHEST
BLOCK = 8


def gll_derivative():
    nodes = np.array([-1.0, -1.0 / np.sqrt(5.0), 1.0 / np.sqrt(5.0), 1.0])
    weights = np.array(
        [1.0 / np.prod([nodes[j] - nodes[k] for k in range(4) if k != j]) for j in range(4)]
    )
    deriv = np.zeros((4, 4))
    for i in range(4):
        for j in range(4):
            if i != j:
                deriv[i, j] = weights[j] / weights[i] / (nodes[i] - nodes[j])
        deriv[i, i] = -deriv[i].sum()
    return 2.0 * deriv


def hat_rows(count_to, count_from):
    dest = (np.arange(count_to) + 0.5) / count_to
    source = (np.arange(count_from) + 0.5) / count_from
    hat = np.maximum(0.0, 1.0 - np.abs(dest[:, None] - source[None, :]) * count_from)
    hat = hat / hat.sum(axis=1, keepdims=True)
    return [[(int(c), float(row[c])) for c in np.nonzero(row > 1e-9)[0]] for row in hat]


def lanes_of(shape):
    return lax.broadcasted_iota(jnp.int32, shape, len(shape) - 1)


def rows_of(shape):
    return lax.broadcasted_iota(jnp.int32, shape, len(shape) - 2)


def fetch(pairs, sems):
    copies = [pltpu.make_async_copy(a, b, sems.at[i]) for i, (a, b) in enumerate(pairs)]
    for copy in copies:
        copy.start()
    return copies


def tendency_kernel(
    levels, hbm_wind_x, hbm_wind_y, hbm_gcm, tend, first, last, low_end, high_end,
    wind_x, wind_y, gcm, sems,
):
    copies = fetch(((hbm_gcm, gcm), (hbm_wind_x, wind_x), (hbm_wind_y, wind_y)), sems)
    deriv = gll_derivative()
    rows, lanes = gcm.shape
    side_a, side_b = rows_of((lanes, lanes)), lanes_of((lanes, lanes))
    step_y = jnp.zeros((lanes, lanes), jnp.float32)
    for m in range(4):
        for n in range(4):
            step_y = jnp.where((side_a % 4 == m) & (side_b % 4 == n), float(deriv[n, m]), step_y)
    step_y = jnp.where(side_a // 4 == side_b // 4, step_y, 0.0)
    for copy in copies:
        copy.wait()
    tend[...] = jnp.dot(gcm[...], step_y, precision=HIGH, preferred_element_type=jnp.float32)
    row = rows_of((8, lanes))
    low = row < 4
    factors = {}
    for shift in range(-3, 4):
        factor = jnp.zeros((8, lanes), jnp.float32)
        for i in range(4):
            if 0 <= i - shift < 4:
                factor = jnp.where(row % 4 == i, float(deriv[i, i - shift]), factor)
        factors[shift] = factor
    for v in range(rows // 8):
        at = slice(8 * v, 8 * v + 8)
        lev = 2 * v % levels
        here = gcm[at, :]
        along_x = factors[0] * here
        for shift in (-3, -2, -1, 1, 2, 3):
            along_x = along_x + factors[shift] * pltpu.roll(here, shift % 8, 0)
        blow_x = jnp.where(low, wind_x[lev], wind_x[lev + 1])
        blow_y = jnp.where(low, wind_y[lev], wind_y[lev + 1])
        tend[at, :] = -(blow_x * along_x + blow_y * tend[at, :])
    count = rows // 4
    first[...] = tend[pl.ds(0, count, stride=4), :]
    last[...] = tend[pl.ds(3, count, stride=4), :]
    pick = jnp.where(
        lanes_of((8, lanes)) == jnp.where(rows_of((8, lanes)) == 0, 0, lanes - 1), 1.0, 0.0
    )
    edge = lax.dot_general(
        pick, tend[...], (((1,), (1,)), ((), ())), precision=HIGH, preferred_element_type=jnp.float32
    )
    for i, end in enumerate((low_end, high_end)):
        end[:, :rows] = edge[i : i + 1]
        end[:, rows:] = jnp.zeros((1, end.shape[1] - rows), jnp.float32)


def dynamic_kernel(
    levels, cloud_levels, hbm_gcm, hbm_tend, hbm_before, hbm_after, hbm_left, hbm_left_before,
    hbm_left_after, hbm_right, hbm_right_before, hbm_right_after, hbm_change, out,
    gcm, tend, work, before, after, ends, change, sems,
):
    sides = (hbm_left, hbm_left_before, hbm_left_after, hbm_right, hbm_right_before, hbm_right_after)
    copies = fetch(
        ((hbm_before, before), (hbm_after, after), (hbm_tend, tend), (hbm_gcm, gcm))
        + tuple((side, ends.at[i]) for i, side in enumerate(sides))
        + ((hbm_change, change),),
        sems,
    )
    for copy in copies:
        copy.wait()
    rows, lanes = gcm.shape
    count = rows // 4
    work[...] = tend[...]
    work[pl.ds(0, count, stride=4), :] = before[...]
    work[pl.ds(3, count, stride=4), :] = after[...]
    width = ends.shape[2]
    lane = lanes_of((1, width))

    def side(base):
        mid, low, high = ends[base], ends[base + 1], ends[base + 2]
        other = jnp.where(
            lane % 4 == 0,
            pltpu.roll(low, width - 3, 1),
            jnp.where(lane % 4 == 3, pltpu.roll(high, 3, 1), mid),
        )
        return 0.5 * (mid + other)

    pair = jnp.concatenate([side(0), side(3), jnp.zeros((6, width), jnp.float32)], axis=0)
    row8, lane8 = rows_of((8, lanes)), lanes_of((8, lanes))
    spread = jnp.where((row8 < 2) & (lane8 == jnp.where(row8 == 0, 0, lanes - 1)), 1.0, 0.0)
    halo = lax.dot_general(
        pair, spread, (((0,), (0,)), ((), ())), precision=HIGH, preferred_element_type=jnp.float32
    )
    low = row8 < 4
    hats = hat_rows(levels, cloud_levels)

    def feedback(field, lev):
        total = None
        for k, weight in hats[lev]:
            term = weight * change[field, k]
            total = term if total is None else total + term
        return total

    for v in range(rows // 8):
        at = slice(8 * v, 8 * v + 8)
        field, lev = divmod(2 * v, levels)
        shared_x = 0.5 * (tend[at, :] + work[at, :])
        beside = jnp.where(
            lane8 % 4 == 0,
            pltpu.roll(shared_x, 1, 1),
            jnp.where(lane8 % 4 == 3, pltpu.roll(shared_x, lanes - 1, 1), shared_x),
        )
        beside = jnp.where((lane8 == 0) | (lane8 == lanes - 1), halo[at, :], beside)
        shared = 0.5 * (shared_x + beside)
        dynamic = gcm[at, :] + DT_DYN * shared
        out[at, :] = dynamic + jnp.where(low, feedback(field, lev), feedback(field, lev + 1))


def cloud_kernel(
    hbm_courant, hbm_relax, hbm_sat, hbm_cond, hbm_gcm, hbm_active, crm, new, change,
    courant, relax, sat, cond_rate, gcm, active,
    held, one, two, fixed, other, begin, profile, sems, in_sem, out_sem,
):
    copies = fetch(
        (
            (hbm_gcm, gcm),
            (hbm_relax, relax),
            (hbm_sat, sat),
            (hbm_courant, courant),
            (hbm_cond, cond_rate),
            (hbm_active, active),
        ),
        sems,
    )
    fields, levels, rows, lanes = crm.shape
    half_tiles = rows // 16
    tiles = rows // 8
    source_levels = profile.shape[1]
    chunk = levels // 2
    low = rows_of((8, lanes)) < 4

    def piece(f, c):
        return pl.ds(c * chunk, chunk)

    loads = [
        pltpu.make_async_copy(
            crm.at[f, pl.ds(c * chunk, chunk)], held.at[f, pl.ds(c * chunk, chunk)], in_sem.at[f, c]
        )
        for f in range(fields)
        for c in range(2)
    ]
    for load in loads:
        load.start()
    for copy in copies:
        copy.wait()

    for f in range(fields):
        for v in range(source_levels // 2):
            base = (f * source_levels + 2 * v) * 4
            pair = gcm[base : base + 8, :].astype(jnp.bfloat16).astype(jnp.float32)
            swapped = pltpu.roll(pair, 4, 0)
            profile[f, 2 * v] = jnp.where(low, pair, swapped)
            profile[f, 2 * v + 1] = jnp.where(low, swapped, pair)
    for k, entries in enumerate(hat_rows(levels, source_levels)):
        for f in range(fields):
            total = None
            for l, weight in entries:
                term = weight * profile[f, l]
                total = term if total is None else total + term
            fixed[f, k] = total

    def forward(k, carry):
        ends = jnp.where((k == 0) | (k == levels - 1), KAPPA, 2.0 * KAPPA)
        result = []
        for f in range(fields):
            ratio, value = carry[f]
            rate = DT_CLOUD * relax[f, k]
            scale = 1.0 / (jnp.full((8, lanes), ends + rate, jnp.float32) - KAPPA * ratio)
            value = (rate * fixed[f, k] + KAPPA * value) * scale
            ratio = KAPPA * scale
            fixed[f, k] = value
            begin[f, k] = ratio
            result.append((ratio, value))
        return tuple(result)

    zero = jnp.zeros((8, lanes), jnp.float32)
    lax.fori_loop(0, levels, forward, tuple((zero, zero) for _ in range(fields)))

    def backward(i, carry):
        k = levels - 1 - i
        result = []
        for f in range(fields):
            value = fixed[f, k] + begin[f, k] * carry[f]
            fixed[f, k] = value
            result.append(value)
        other[k] = result[1] - sat[k]
        return tuple(result)

    lax.fori_loop(0, levels, backward, tuple(zero for _ in range(fields)))

    def unpack(f):
        def at(k, _):
            block = held[f, k].astype(jnp.float32)
            steady = fixed[f, k]
            total = zero
            for u in range(half_tiles):
                near, far = block[8 * u : 8 * u + 8], block[8 * (u + half_tiles) : 8 * (u + half_tiles) + 8]
                even = jnp.where(low, near, pltpu.roll(far, 4, 0))
                odd = jnp.where(low, pltpu.roll(near, 4, 0), far)
                total = total + (even + odd)
                one[f, k, 16 * u : 16 * u + 8, :] = even - steady
                one[f, k, 16 * u + 8 : 16 * u + 16, :] = odd - steady
            begin[f, k] = total
            return 0

        return at

    for i, load in enumerate(loads):
        load.wait()
        f, c = divmod(i, 2)
        lax.fori_loop(c * chunk, (c + 1) * chunk, unpack(f), 0)

    def advance(src, dst, first, count, scale, inverse):
        ks = [first + i for i in range(count)]
        reach = [jnp.maximum(first - 1, 0)] + ks + [jnp.minimum(first + count, levels - 1)]
        shift = [courant[k] * (1.0 / KAPPA) for k in ks]
        keep = [
            [
                (1.0 - 2.0 * KAPPA - courant[k] - DT_CLOUD * relax[f, k]) * (1.0 / KAPPA)
                for k in ks
            ]
            for f in range(fields)
        ]
        rate = [DT_CLOUD * cond_rate[k] * inverse for k in ks]
        offset = [other[k] for k in ks]
        left = [
            [pltpu.roll(src[f, k, rows - 8 : rows, :], 4, 0) for k in ks] for f in range(fields)
        ]
        for w in range(tiles):
            at = slice(8 * w, 8 * w + 8)
            here = [[src[f, k, at, :] for k in reach] for f in range(fields)]
            for i, k in enumerate(ks):
                condense = rate[i] * jnp.tanh(here[1][i + 1] * scale + offset[i])
                for f in range(fields):
                    moved = (here[f][i] + here[f][i + 2]) + (
                        keep[f][i] * here[f][i + 1] + shift[i] * left[f][i]
                    )
                    dst[f, k, at, :] = moved + condense if f == 0 else moved - condense
            left = [here[f][1:-1] for f in range(fields)]

    def substep(src, dst, scale, inverse):
        whole = levels // BLOCK

        def step(b, _):
            advance(src, dst, b * BLOCK, BLOCK, scale, inverse)
            return 0

        lax.fori_loop(0, whole, step, 0)
        if levels % BLOCK:
            advance(src, dst, whole * BLOCK, levels % BLOCK, scale, inverse)

    def two_substeps(_, carry):
        scale, inverse = carry
        substep(one, two, scale, inverse)
        scale, inverse = scale * KAPPA, inverse * (1.0 / KAPPA)
        substep(two, one, scale, inverse)
        return scale * KAPPA, inverse * (1.0 / KAPPA)

    final, _ = lax.fori_loop(
        0, SUBSTEPS // 2, two_substeps, (jnp.float32(1.0), jnp.float32(1.0 / KAPPA))
    )

    chosen = jnp.concatenate([active[...], active[...]], axis=0) > 0
    share = 2.0 / rows * 2.0

    def pack(f):
        def at(k, _):
            steady = fixed[f, k]
            block = held[f, k].astype(jnp.float32)
            total = zero
            near, far = [], []
            for u in range(half_tiles):
                even = one[f, k, 16 * u : 16 * u + 8, :] * final + steady
                odd = one[f, k, 16 * u + 8 : 16 * u + 16, :] * final + steady
                total = total + (even + odd)
                near.append(jnp.where(low, even, pltpu.roll(odd, 4, 0)))
                far.append(jnp.where(low, pltpu.roll(even, 4, 0), odd))
            tiles_new = [
                jnp.where(chosen, tile, block[8 * u : 8 * u + 8]) for u, tile in enumerate(near + far)
            ]
            held[f, k] = jnp.concatenate(tiles_new, axis=0).astype(jnp.bfloat16)
            total = total - begin[f, k]
            total = (total + pltpu.roll(total, 4, 0)) * share
            total = total.astype(jnp.bfloat16).astype(jnp.float32)
            change[f, k] = jnp.where(chosen, total, 0.0)
            return 0

        return at

    stores = []
    for f in range(fields):
        for c in range(2):
            lax.fori_loop(c * chunk, (c + 1) * chunk, pack(f), 0)
            store = pltpu.make_async_copy(
                held.at[f, pl.ds(c * chunk, chunk)], new.at[f, pl.ds(c * chunk, chunk)], out_sem.at[f, c]
            )
            store.start()
            stores.append(store)
    for store in stores:
        store.wait()


def body(gcm_state, crm_state, active, wind_x, wind_y, courant, relax, sat, cond_rate):
    fields, levels, rows_x, lanes = gcm_state.shape
    cloud_levels, cloud_columns = crm_state.shape[1:3]
    rows = fields * levels * rows_x
    gcm = gcm_state.reshape(rows, lanes)
    crm = crm_state.reshape(fields, cloud_levels, cloud_columns * rows_x, lanes)
    def kept(*arrays):
        return [pltpu.with_memory_space_constraint(a, pltpu.HBM) for a in arrays]

    vmem = pl.BlockSpec(memory_space=pltpu.VMEM)
    anywhere = pl.BlockSpec(memory_space=pl.ANY)
    hbm = pl.BlockSpec(memory_space=pltpu.HBM)
    dma = pltpu.SemaphoreType.DMA
    f32 = jnp.float32
    count = rows // rows_x
    width = (rows + 127) // 128 * 128

    tend, first, last, low_end, high_end = pl.pallas_call(
        functools.partial(tendency_kernel, levels),
        out_shape=(
            jax.ShapeDtypeStruct((rows, lanes), f32),
            jax.ShapeDtypeStruct((count, lanes), f32),
            jax.ShapeDtypeStruct((count, lanes), f32),
            jax.ShapeDtypeStruct((1, width), f32),
            jax.ShapeDtypeStruct((1, width), f32),
        ),
        in_specs=[hbm] * 3,
        out_specs=(vmem,) * 5,
        scratch_shapes=[
            pltpu.SMEM(wind_x.shape, f32),
            pltpu.SMEM(wind_y.shape, f32),
            pltpu.VMEM((rows, lanes), f32),
            dma((3,)),
        ],
        name="tendency",
    )(*kept(wind_x, wind_y, gcm))

    count_x, count_y = lax.axis_size("col"), lax.axis_size("sub")

    def moved(cells, dx, dy):
        if dy == 0:
            return lax.ppermute(cells, "col", [(i, (i + dx) % count_x) for i in range(count_x)])
        if dx == 0:
            return lax.ppermute(cells, "sub", [(i, (i + dy) % count_y) for i in range(count_y)])
        pairs = [
            (i * count_y + j, (i + dx) % count_x * count_y + (j + dy) % count_y)
            for i in range(count_x)
            for j in range(count_y)
        ]
        return lax.ppermute(cells, ("col", "sub"), pairs)

    before, after = moved(last, 1, 0), moved(first, -1, 0)
    sides = [moved(high_end, dx, 1) for dx in (0, 1, -1)]
    sides += [moved(low_end, dx, -1) for dx in (0, 1, -1)]

    slots = (fields, cloud_levels, cloud_columns * rows_x, lanes)
    tile = (fields, cloud_levels, 8, lanes)
    new, change = pl.pallas_call(
        cloud_kernel,
        out_shape=(jax.ShapeDtypeStruct(slots, jnp.bfloat16), jax.ShapeDtypeStruct(tile, f32)),
        in_specs=[hbm] * 7,
        out_specs=(hbm, vmem),
        scratch_shapes=[
            pltpu.SMEM(courant.shape, f32),
            pltpu.SMEM(relax.shape, f32),
            pltpu.SMEM(sat.shape, f32),
            pltpu.SMEM(cond_rate.shape, f32),
            pltpu.VMEM((rows, lanes), f32),
            pltpu.VMEM(active.shape, active.dtype),
            pltpu.VMEM(slots, jnp.bfloat16),
            pltpu.VMEM(slots, f32),
            pltpu.VMEM(slots, f32),
            pltpu.VMEM(tile, f32),
            pltpu.VMEM(tile[1:], f32),
            pltpu.VMEM(tile, f32),
            pltpu.VMEM((fields, levels, 8, lanes), f32),
            dma((6,)),
            dma((fields, 2)),
            dma((fields, 2)),
        ],
        compiler_params=pltpu.CompilerParams(vmem_limit_bytes=48 << 20),
        cost_estimate=pl.CostEstimate(
            flops=60_000_000, bytes_accessed=200_000_000, transcendentals=20_000_000
        ),
        name="cloud",
    )(*kept(courant, relax, sat, cond_rate, gcm, active, crm))

    out = pl.pallas_call(
        functools.partial(dynamic_kernel, levels, cloud_levels),
        out_shape=jax.ShapeDtypeStruct((rows, lanes), f32),
        in_specs=[hbm] + [anywhere] * 10,
        out_specs=vmem,
        scratch_shapes=[
            pltpu.VMEM((rows, lanes), f32),
            pltpu.VMEM((rows, lanes), f32),
            pltpu.VMEM((rows, lanes), f32),
            pltpu.VMEM((count, lanes), f32),
            pltpu.VMEM((count, lanes), f32),
            pltpu.VMEM((6, 1, width), f32),
            pltpu.VMEM(tile, f32),
            dma((11,)),
        ],
        name="dynamic",
    )(*kept(gcm), tend, before, after, *sides, change)
    return out.reshape(gcm_state.shape), new.reshape(crm_state.shape)


def solution(mesh):
    placed = (
        P(None, None, ("groups", "col"), "sub"),
        P(None, None, None, ("groups", "col"), "sub"),
        P(("groups", "col"), "sub"),
        P(),
        P(),
        P(),
        P(),
        P(),
        P(),
    )
    return jax.shard_map(
        body,
        mesh=mesh,
        in_specs=placed,
        out_specs=(
            P(None, None, ("groups", "col"), "sub"),
            P(None, None, None, ("groups", "col"), "sub"),
        ),
        check_vma=False,
    )
```

```python
import functools

import jax
import jax.numpy as jnp
import numpy as np
from jax import lax
from jax.experimental import pallas as pl
from jax.experimental.pallas import tpu as pltpu
from jax.sharding import PartitionSpec as P

SUBSTEPS = 24
DT_DYN = 0.05
DT_CLOUD = 0.5
KAPPA = 0.15
HIGH = lax.Precision.HIGHEST
BLOCK = 8
PIECES = 4


def gll_derivative():
    nodes = np.array([-1.0, -1.0 / np.sqrt(5.0), 1.0 / np.sqrt(5.0), 1.0])
    weights = np.array(
        [1.0 / np.prod([nodes[j] - nodes[k] for k in range(4) if k != j]) for j in range(4)]
    )
    deriv = np.zeros((4, 4))
    for i in range(4):
        for j in range(4):
            if i != j:
                deriv[i, j] = weights[j] / weights[i] / (nodes[i] - nodes[j])
        deriv[i, i] = -deriv[i].sum()
    return 2.0 * deriv


def hat_rows(count_to, count_from):
    dest = (np.arange(count_to) + 0.5) / count_to
    source = (np.arange(count_from) + 0.5) / count_from
    hat = np.maximum(0.0, 1.0 - np.abs(dest[:, None] - source[None, :]) * count_from)
    hat = hat / hat.sum(axis=1, keepdims=True)
    return [[(int(c), float(row[c])) for c in np.nonzero(row > 1e-9)[0]] for row in hat]


def lanes_of(shape):
    return lax.broadcasted_iota(jnp.int32, shape, len(shape) - 1)


def rows_of(shape):
    return lax.broadcasted_iota(jnp.int32, shape, len(shape) - 2)


def fetch(pairs, sems):
    copies = [pltpu.make_async_copy(a, b, sems.at[i]) for i, (a, b) in enumerate(pairs)]
    for copy in copies:
        copy.start()
    return copies


def along_lanes(lanes):
    deriv = gll_derivative()
    side_a, side_b = rows_of((lanes, lanes)), lanes_of((lanes, lanes))
    step = jnp.zeros((lanes, lanes), jnp.float32)
    for m in range(4):
        for n in range(4):
            step = jnp.where((side_a % 4 == m) & (side_b % 4 == n), float(deriv[n, m]), step)
    return jnp.where(side_a // 4 == side_b // 4, step, 0.0)


def tendency(levels, wind_x, wind_y, gcm, tend):
    deriv = gll_derivative()
    rows, lanes = gcm.shape
    tend[...] = jnp.dot(
        gcm[...], along_lanes(lanes), precision=HIGH, preferred_element_type=jnp.float32
    )
    row = rows_of((8, lanes))
    low = row < 4
    factors = {}
    for shift in range(-3, 4):
        factor = jnp.zeros((8, lanes), jnp.float32)
        for i in range(4):
            if 0 <= i - shift < 4:
                factor = jnp.where(row % 4 == i, float(deriv[i, i - shift]), factor)
        factors[shift] = factor
    for v in range(rows // 8):
        at = slice(8 * v, 8 * v + 8)
        lev = 2 * v % levels
        here = gcm[at, :]
        along_x = factors[0] * here
        for shift in (-3, -2, -1, 1, 2, 3):
            along_x = along_x + factors[shift] * pltpu.roll(here, shift % 8, 0)
        blow_x = jnp.where(low, wind_x[lev], wind_x[lev + 1])
        blow_y = jnp.where(low, wind_y[lev], wind_y[lev + 1])
        tend[at, :] = -(blow_x * along_x + blow_y * tend[at, :])


def share_kernel(
    levels, hbm_wind_x, hbm_wind_y, hbm_before, hbm_after, hbm_tend, shared, low_end, high_end,
    wind_x, wind_y, before, after, tend, work, blow, sems,
):
    copies = fetch(
        (
            (hbm_before, before),
            (hbm_after, after),
            (hbm_tend, tend),
            (hbm_wind_x, wind_x),
            (hbm_wind_y, wind_y),
        ),
        sems,
    )
    deriv = gll_derivative()
    rows, lanes = tend.shape
    fields = rows // (4 * levels)
    step = along_lanes(lanes)
    low = rows_of((8, lanes)) < 4
    for copy in copies:
        copy.wait()
    for v in range(levels // 2):
        at = slice(8 * v, 8 * v + 8)
        blow[0, at, :] = jnp.where(low, wind_x[2 * v], wind_x[2 * v + 1])
        blow[1, at, :] = jnp.where(low, wind_y[2 * v], wind_y[2 * v + 1])
    blow_x = blow[0, pl.ds(0, levels, stride=4), :]
    blow_y = blow[1, pl.ds(0, levels, stride=4), :]
    work[...] = tend[...]
    for f in range(fields):
        for cells, node, dest in ((before, 3, 0), (after, 0, 3)):
            nodes = [cells[pl.ds(4 * levels * f + m, levels, stride=4), :] for m in range(4)]
            along_x = sum(float(deriv[node, m]) * nodes[m] for m in range(4))
            along_y = jnp.dot(
                nodes[node], step, precision=HIGH, preferred_element_type=jnp.float32
            )
            work[pl.ds(4 * levels * f + dest, levels, stride=4), :] = -(
                blow_x * along_x + blow_y * along_y
            )
    work[...] = 0.5 * (tend[...] + work[...])
    shared[...] = work[...]
    pick = jnp.where(
        lanes_of((8, lanes)) == jnp.where(rows_of((8, lanes)) == 0, 0, lanes - 1), 1.0, 0.0
    )
    edge = lax.dot_general(
        pick, work[...], (((1,), (1,)), ((), ())), precision=HIGH, preferred_element_type=jnp.float32
    )
    for i, end in enumerate((low_end, high_end)):
        end[:, :rows] = edge[i : i + 1]
        end[:, rows:] = jnp.zeros((1, end.shape[1] - rows), jnp.float32)


def dynamic_kernel(
    levels, cloud_levels, hbm_gcm, hbm_shared, hbm_left, hbm_right, hbm_change, out,
    gcm, shared, left, right, change, sems,
):
    copies = fetch(
        (
            (hbm_gcm, gcm),
            (hbm_shared, shared),
            (hbm_left, left),
            (hbm_right, right),
            (hbm_change, change),
        ),
        sems,
    )
    for copy in copies:
        copy.wait()
    rows, lanes = gcm.shape
    width = left.shape[1]
    pair = jnp.concatenate([left[...], right[...], jnp.zeros((6, width), jnp.float32)], axis=0)
    row8, lane8 = rows_of((8, lanes)), lanes_of((8, lanes))
    spread = jnp.where((row8 < 2) & (lane8 == jnp.where(row8 == 0, 0, lanes - 1)), 1.0, 0.0)
    halo = lax.dot_general(
        pair, spread, (((0,), (0,)), ((), ())), precision=HIGH, preferred_element_type=jnp.float32
    )
    low = row8 < 4
    hats = hat_rows(levels, cloud_levels)

    def feedback(field, lev):
        total = None
        for k, weight in hats[lev]:
            term = weight * change[field, k]
            total = term if total is None else total + term
        return total

    for v in range(rows // 8):
        at = slice(8 * v, 8 * v + 8)
        field, lev = divmod(2 * v, levels)
        here = shared[at, :]
        beside = jnp.where(
            lane8 % 4 == 0,
            pltpu.roll(here, 1, 1),
            jnp.where(lane8 % 4 == 3, pltpu.roll(here, lanes - 1, 1), here),
        )
        beside = jnp.where((lane8 == 0) | (lane8 == lanes - 1), halo[at, :], beside)
        dynamic = gcm[at, :] + DT_DYN * (0.5 * (here + beside))
        out[at, :] = dynamic + jnp.where(low, feedback(field, lev), feedback(field, lev + 1))


def cloud_kernel(
    hbm_courant, hbm_relax, hbm_sat, hbm_cond, hbm_gcm, hbm_active, hbm_wind_x, hbm_wind_y, crm,
    new, hbm_change, hbm_tend,
    courant, relax, sat, cond_rate, gcm, active, wind_x, wind_y, change, tend,
    held, one, two, fixed, other, begin, profile, sems, in_sem, out_sem, late_sem,
):
    copies = fetch(
        (
            (hbm_gcm, gcm),
            (hbm_relax, relax),
            (hbm_sat, sat),
            (hbm_courant, courant),
            (hbm_cond, cond_rate),
            (hbm_active, active),
            (hbm_wind_x, wind_x),
            (hbm_wind_y, wind_y),
        ),
        sems,
    )
    fields, levels, rows, lanes = crm.shape
    half_tiles = rows // 16
    tiles = rows // 8
    source_levels = profile.shape[1]
    cuts = [levels * c // (2 * PIECES) * 2 for c in range(PIECES)] + [levels]
    pieces = [pl.ds(a, b - a) for a, b in zip(cuts[:-1], cuts[1:])]
    low = rows_of((8, lanes)) < 4

    loads = [
        [
            pltpu.make_async_copy(crm.at[f, piece], held.at[f, piece], in_sem.at[f, c])
            for f in range(fields)
        ]
        for c, piece in enumerate(pieces)
    ]
    for group in loads[::-1]:
        for load in group:
            load.start()
    for copy in copies:
        copy.wait()

    for f in range(fields):
        for v in range(source_levels // 2):
            base = (f * source_levels + 2 * v) * 4
            pair = gcm[base : base + 8, :].astype(jnp.bfloat16).astype(jnp.float32)
            swapped = pltpu.roll(pair, 4, 0)
            profile[f, 2 * v] = jnp.where(low, pair, swapped)
            profile[f, 2 * v + 1] = jnp.where(low, swapped, pair)
    for k, entries in enumerate(hat_rows(levels, source_levels)):
        for f in range(fields):
            total = None
            for l, weight in entries:
                term = weight * profile[f, l]
                total = term if total is None else total + term
            fixed[f, k] = total

    zero = jnp.zeros((8, lanes), jnp.float32)
    ratio, value = [zero] * fields, [zero] * fields
    for k in range(levels):
        ends = KAPPA if k in (0, levels - 1) else 2.0 * KAPPA
        for f in range(fields):
            rate = DT_CLOUD * relax[f, k]
            scale = 1.0 / (jnp.full((8, lanes), ends + rate, jnp.float32) - KAPPA * ratio[f])
            value[f] = (rate * fixed[f, k] + KAPPA * value[f]) * scale
            ratio[f] = KAPPA * scale
            fixed[f, k] = value[f]
            begin[f, k] = ratio[f]
    tendency(source_levels, wind_x, wind_y, gcm, tend)
    late = [pltpu.make_async_copy(tend, hbm_tend, late_sem.at[0])]
    late[0].start()

    def unpack(i, carry):
        k = levels - 1 - i
        result = []
        for f in range(fields):
            steady = fixed[f, k] + begin[f, k] * carry[f]
            fixed[f, k] = steady
            result.append(steady)
            block = held[f, k].astype(jnp.float32)
            total = zero
            for u in range(half_tiles):
                near, far = (block[8 * t : 8 * t + 8] for t in (u, u + half_tiles))
                even = jnp.where(low, near, pltpu.roll(far, 4, 0))
                odd = jnp.where(low, pltpu.roll(near, 4, 0), far)
                total = total + (even + odd)
                one[f, k, 16 * u : 16 * u + 8, :] = even - steady
                one[f, k, 16 * u + 8 : 16 * u + 16, :] = odd - steady
            begin[f, k] = total
        other[k] = result[1] - sat[k]
        return tuple(result)

    carry = (zero,) * fields
    for c in range(PIECES - 1, -1, -1):
        for load in loads[c]:
            load.wait()
        first, last = levels - cuts[c + 1], levels - cuts[c]
        carry = lax.fori_loop(first, last, unpack, carry, unroll=2)

    def advance(src, dst, first, count, scale, inverse):
        ks = [first + i for i in range(count)]
        reach = [jnp.maximum(first - 1, 0)] + ks + [jnp.minimum(first + count, levels - 1)]
        shift = [courant[k] * (1.0 / KAPPA) for k in ks]
        keep = [
            [
                (1.0 - 2.0 * KAPPA - courant[k] - DT_CLOUD * relax[f, k]) * (1.0 / KAPPA)
                for k in ks
            ]
            for f in range(fields)
        ]
        rate = [DT_CLOUD * cond_rate[k] * inverse for k in ks]
        offset = [other[k] for k in ks]
        left = [
            [pltpu.roll(src[f, k, rows - 8 : rows, :], 4, 0) for k in ks] for f in range(fields)
        ]
        for w in range(tiles):
            at = slice(8 * w, 8 * w + 8)
            here = [[src[f, k, at, :] for k in reach] for f in range(fields)]
            for i, k in enumerate(ks):
                condense = rate[i] * jnp.tanh(here[1][i + 1] * scale + offset[i])
                for f in range(fields):
                    moved = (here[f][i] + here[f][i + 2]) + (
                        keep[f][i] * here[f][i + 1] + shift[i] * left[f][i]
                    )
                    dst[f, k, at, :] = moved + condense if f == 0 else moved - condense
            left = [here[f][1:-1] for f in range(fields)]

    def substep(src, dst, scale, inverse):
        whole = levels // BLOCK

        def step(b, _):
            advance(src, dst, b * BLOCK, BLOCK, scale, inverse)
            return 0

        lax.fori_loop(0, whole, step, 0)
        if levels % BLOCK:
            advance(src, dst, whole * BLOCK, levels % BLOCK, scale, inverse)

    def two_substeps(_, carry):
        scale, inverse = carry
        substep(one, two, scale, inverse)
        scale, inverse = scale * KAPPA, inverse * (1.0 / KAPPA)
        substep(two, one, scale, inverse)
        return scale * KAPPA, inverse * (1.0 / KAPPA)

    final, _ = lax.fori_loop(
        0, SUBSTEPS // 2, two_substeps, (jnp.float32(1.0), jnp.float32(1.0 / KAPPA))
    )

    chosen = jnp.concatenate([active[...], active[...]], axis=0) > 0
    chosen16 = jnp.concatenate([active[...]] * 4, axis=0).astype(jnp.bfloat16) > 0
    share = 4.0 / rows

    def pack(f):
        def at(k, _):
            steady = fixed[f, k]
            total = zero
            near, far = [], []
            for u in range(half_tiles):
                even = one[f, k, 16 * u : 16 * u + 8, :] * final + steady
                odd = one[f, k, 16 * u + 8 : 16 * u + 16, :] * final + steady
                total = total + (even + odd)
                near.append(jnp.where(low, even, pltpu.roll(odd, 4, 0)))
                far.append(jnp.where(low, pltpu.roll(even, 4, 0), odd))
            tiles_new = near + far
            for u in range(half_tiles):
                pair = jnp.concatenate(tiles_new[2 * u : 2 * u + 2], axis=0).astype(jnp.bfloat16)
                at16 = slice(16 * u, 16 * u + 16)
                held[f, k, at16, :] = jnp.where(chosen16, pair, held[f, k, at16, :])
            total = total - begin[f, k]
            total = (total + pltpu.roll(total, 4, 0)) * share
            total = total.astype(jnp.bfloat16).astype(jnp.float32)
            change[f, k] = jnp.where(chosen, total, 0.0)
            return 0

        return at

    for c, piece in enumerate(pieces):
        for f in range(fields):
            lax.fori_loop(cuts[c], cuts[c + 1], pack(f), 0, unroll=2)
            store = pltpu.make_async_copy(held.at[f, piece], new.at[f, piece], out_sem.at[f, c])
            store.start()
            late.append(store)
    store = pltpu.make_async_copy(change, hbm_change, late_sem.at[1])
    store.start()
    late.append(store)
    for store in late:
        store.wait()


def body(gcm_state, crm_state, active, wind_x, wind_y, courant, relax, sat, cond_rate):
    fields, levels, rows_x, lanes = gcm_state.shape
    cloud_levels, cloud_columns = crm_state.shape[1:3]
    rows = fields * levels * rows_x
    gcm = gcm_state.reshape(rows, lanes)
    crm = crm_state.reshape(fields, cloud_levels, cloud_columns * rows_x, lanes)
    def kept(*arrays):
        return [pltpu.with_memory_space_constraint(a, pltpu.HBM) for a in arrays]

    vmem = pl.BlockSpec(memory_space=pltpu.VMEM)
    anywhere = pl.BlockSpec(memory_space=pl.ANY)
    hbm = pl.BlockSpec(memory_space=pltpu.HBM)
    dma = pltpu.SemaphoreType.DMA
    f32 = jnp.float32
    width = (rows + 127) // 128 * 128

    def moved(cells, axis, step):
        size = lax.axis_size(axis)
        return lax.ppermute(cells, axis, [(i, (i + step) % size) for i in range(size)])

    before, after = moved(gcm, "col", 1), moved(gcm, "col", -1)

    slots = (fields, cloud_levels, cloud_columns * rows_x, lanes)
    tile = (fields, cloud_levels, 8, lanes)
    new, change, tend = pl.pallas_call(
        cloud_kernel,
        out_shape=(
            pltpu.HBM(slots, jnp.bfloat16),
            pltpu.HBM(tile, f32),
            pltpu.HBM((rows, lanes), f32),
        ),
        in_specs=[hbm] * 9,
        out_specs=(hbm,) * 3,
        scratch_shapes=[
            pltpu.SMEM(courant.shape, f32),
            pltpu.SMEM(relax.shape, f32),
            pltpu.SMEM(sat.shape, f32),
            pltpu.SMEM(cond_rate.shape, f32),
            pltpu.VMEM((rows, lanes), f32),
            pltpu.VMEM(active.shape, active.dtype),
            pltpu.SMEM(wind_x.shape, f32),
            pltpu.SMEM(wind_y.shape, f32),
            pltpu.VMEM(tile, f32),
            pltpu.VMEM((rows, lanes), f32),
            pltpu.VMEM(slots, jnp.bfloat16),
            pltpu.VMEM(slots, f32),
            pltpu.VMEM(slots, f32),
            pltpu.VMEM(tile, f32),
            pltpu.VMEM(tile[1:], f32),
            pltpu.VMEM(tile, f32),
            pltpu.VMEM((fields, levels, 8, lanes), f32),
            dma((8,)),
            dma((fields, PIECES)),
            dma((fields, PIECES)),
            dma((2,)),
        ],
        compiler_params=pltpu.CompilerParams(vmem_limit_bytes=48 << 20),
        cost_estimate=pl.CostEstimate(
            flops=60_000_000, bytes_accessed=200_000_000, transcendentals=20_000_000
        ),
        name="cloud",
    )(*kept(courant, relax, sat, cond_rate, gcm, active, wind_x, wind_y, crm))

    shared, low_end, high_end = pl.pallas_call(
        functools.partial(share_kernel, levels),
        out_shape=(
            jax.ShapeDtypeStruct((rows, lanes), f32),
            jax.ShapeDtypeStruct((1, width), f32),
            jax.ShapeDtypeStruct((1, width), f32),
        ),
        in_specs=[hbm] * 5,
        out_specs=(vmem,) * 3,
        scratch_shapes=[
            pltpu.SMEM(wind_x.shape, f32),
            pltpu.SMEM(wind_y.shape, f32),
            pltpu.VMEM((rows, lanes), f32),
            pltpu.VMEM((rows, lanes), f32),
            pltpu.VMEM((rows, lanes), f32),
            pltpu.VMEM((rows, lanes), f32),
            pltpu.VMEM((2, levels * rows_x, lanes), f32),
            dma((5,)),
        ],
        name="share",
    )(*kept(wind_x, wind_y, before, after, tend))
    left, right = moved(high_end, "sub", 1), moved(low_end, "sub", -1)

    out = pl.pallas_call(
        functools.partial(dynamic_kernel, levels, cloud_levels),
        out_shape=jax.ShapeDtypeStruct((rows, lanes), f32),
        in_specs=[hbm] + [anywhere] * 3 + [hbm],
        out_specs=vmem,
        scratch_shapes=[
            pltpu.VMEM((rows, lanes), f32),
            pltpu.VMEM((rows, lanes), f32),
            pltpu.VMEM((1, width), f32),
            pltpu.VMEM((1, width), f32),
            pltpu.VMEM(tile, f32),
            dma((5,)),
        ],
        name="dynamic",
    )(*kept(gcm), shared, left, right, *kept(change))
    return out.reshape(gcm_state.shape), new.reshape(crm_state.shape)


def solution(mesh):
    placed = (
        P(None, None, ("groups", "col"), "sub"),
        P(None, None, None, ("groups", "col"), "sub"),
        P(("groups", "col"), "sub"),
        P(),
        P(),
        P(),
        P(),
        P(),
        P(),
    )
    return jax.shard_map(
        body,
        mesh=mesh,
        in_specs=placed,
        out_specs=(
            P(None, None, ("groups", "col"), "sub"),
            P(None, None, None, ("groups", "col"), "sub"),
        ),
        check_vma=False,
    )
```

```python
import functools

import jax
import jax.numpy as jnp
import numpy as np
from jax import lax
from jax.experimental import pallas as pl
from jax.experimental.pallas import tpu as pltpu
from jax.sharding import PartitionSpec as P

SUBSTEPS = 24
DT_DYN = 0.05
DT_CLOUD = 0.5
KAPPA = 0.15
HIGH = lax.Precision.HIGHEST
GROUP = 4
PIECES = 1


def gll_derivative():
    nodes = np.array([-1.0, -1.0 / np.sqrt(5.0), 1.0 / np.sqrt(5.0), 1.0])
    weights = np.array(
        [1.0 / np.prod([nodes[j] - nodes[k] for k in range(4) if k != j]) for j in range(4)]
    )
    deriv = np.zeros((4, 4))
    for i in range(4):
        for j in range(4):
            if i != j:
                deriv[i, j] = weights[j] / weights[i] / (nodes[i] - nodes[j])
        deriv[i, i] = -deriv[i].sum()
    return 2.0 * deriv


def hat_rows(count_to, count_from):
    dest = (np.arange(count_to) + 0.5) / count_to
    source = (np.arange(count_from) + 0.5) / count_from
    hat = np.maximum(0.0, 1.0 - np.abs(dest[:, None] - source[None, :]) * count_from)
    hat = hat / hat.sum(axis=1, keepdims=True)
    return [[(int(c), float(row[c])) for c in np.nonzero(row > 1e-9)[0]] for row in hat]


def lanes_of(shape):
    return lax.broadcasted_iota(jnp.int32, shape, len(shape) - 1)


def rows_of(shape):
    return lax.broadcasted_iota(jnp.int32, shape, len(shape) - 2)


def fetch(pairs, sems):
    copies = [pltpu.make_async_copy(a, b, sems.at[i]) for i, (a, b) in enumerate(pairs)]
    for copy in copies:
        copy.start()
    return copies


def split_dot(dot, values, ones, dims):
    ones = ones.astype(jnp.bfloat16)
    total = None
    for _ in range(3):
        part = values.astype(jnp.bfloat16)
        values = values - part.astype(jnp.float32)
        term = dot(part, ones, dims, preferred_element_type=jnp.float32)
        total = term if total is None else total + term
    return total


def along_lanes(lanes):
    deriv = gll_derivative()
    side_a, side_b = rows_of((lanes, lanes)), lanes_of((lanes, lanes))
    step = jnp.zeros((lanes, lanes), jnp.float32)
    for m in range(4):
        for n in range(4):
            step = jnp.where((side_a % 4 == m) & (side_b % 4 == n), float(deriv[n, m]), step)
    return jnp.where(side_a // 4 == side_b // 4, step, 0.0)


def tendency(levels, wind_x, wind_y, gcm, tend):
    deriv = gll_derivative()
    rows, lanes = gcm.shape
    tend[...] = jnp.dot(
        gcm[...], along_lanes(lanes), precision=HIGH, preferred_element_type=jnp.float32
    )
    row = rows_of((8, lanes))
    low = row < 4
    factors = {}
    for shift in range(-3, 4):
        factor = jnp.zeros((8, lanes), jnp.float32)
        for i in range(4):
            if 0 <= i - shift < 4:
                factor = jnp.where(row % 4 == i, float(deriv[i, i - shift]), factor)
        factors[shift] = factor
    for v in range(rows // 8):
        at = slice(8 * v, 8 * v + 8)
        lev = 2 * v % levels
        here = gcm[at, :]
        along_x = factors[0] * here
        for shift in (-3, -2, -1, 1, 2, 3):
            along_x = along_x + factors[shift] * pltpu.roll(here, shift % 8, 0)
        blow_x = jnp.where(low, wind_x[lev], wind_x[lev + 1])
        blow_y = jnp.where(low, wind_y[lev], wind_y[lev + 1])
        tend[at, :] = -(blow_x * along_x + blow_y * tend[at, :])


def share_kernel(
    levels, hbm_wind_x, hbm_wind_y, hbm_before, hbm_after, hbm_tend, shared, low_end, high_end,
    wind_x, wind_y, before, after, tend, work, blow, sems,
):
    copies = fetch(
        (
            (hbm_wind_x, wind_x),
            (hbm_wind_y, wind_y),
            (hbm_before, before),
            (hbm_after, after),
            (hbm_tend, tend),
        ),
        sems,
    )
    deriv = gll_derivative()
    rows, lanes = tend.shape
    fields = rows // (4 * levels)
    step = along_lanes(lanes)
    low = rows_of((8, lanes)) < 4
    for copy in copies[:2]:
        copy.wait()
    for v in range(levels // 2):
        at = slice(8 * v, 8 * v + 8)
        blow[0, at, :] = jnp.where(low, wind_x[2 * v], wind_x[2 * v + 1])
        blow[1, at, :] = jnp.where(low, wind_y[2 * v], wind_y[2 * v + 1])
    blow_x = blow[0, pl.ds(0, levels, stride=4), :]
    blow_y = blow[1, pl.ds(0, levels, stride=4), :]
    for copy in copies[2:]:
        copy.wait()
    work[...] = tend[...]
    for f in range(fields):
        for cells, node, dest in ((before, 3, 0), (after, 0, 3)):
            nodes = [cells[pl.ds(4 * levels * f + m, levels, stride=4), :] for m in range(4)]
            along_x = sum(float(deriv[node, m]) * nodes[m] for m in range(4))
            along_y = jnp.dot(
                nodes[node], step, precision=HIGH, preferred_element_type=jnp.float32
            )
            work[pl.ds(4 * levels * f + dest, levels, stride=4), :] = -(
                blow_x * along_x + blow_y * along_y
            )
    work[...] = 0.5 * (tend[...] + work[...])
    shared[...] = work[...]
    pick = jnp.where(
        lanes_of((8, lanes)) == jnp.where(rows_of((8, lanes)) == 0, 0, lanes - 1), 1.0, 0.0
    )
    edge = split_dot(
        lambda a, b, dims, **kw: lax.dot_general(b, a, dims, **kw),
        work[...], pick, (((1,), (1,)), ((), ())),
    )
    for i, end in enumerate((low_end, high_end)):
        end[:, :rows] = edge[i : i + 1]
        end[:, rows:] = jnp.zeros((1, end.shape[1] - rows), jnp.float32)


def inner_kernel(
    levels, cloud_levels, hbm_gcm, hbm_shared, hbm_change, out, gcm, shared, change, sems
):
    copies = fetch(((hbm_shared, shared), (hbm_gcm, gcm), (hbm_change, change)), sems)
    for copy in copies:
        copy.wait()
    rows, lanes = gcm.shape
    row8, lane8 = rows_of((8, lanes)), lanes_of((8, lanes))
    first, last = lane8 % 4 == 0, lane8 % 4 == 3
    outer = (lane8 == 0) | (lane8 == lanes - 1)
    low = row8 < 4
    hats = hat_rows(levels, cloud_levels)

    def feedback(field, lev):
        total = None
        for k, weight in hats[lev]:
            term = weight * change[field, k]
            total = term if total is None else total + term
        return total

    for v in range(rows // 8):
        at = slice(8 * v, 8 * v + 8)
        here = shared[at, :]
        beside = jnp.where(
            first,
            pltpu.roll(here, 1, 1),
            jnp.where(last, pltpu.roll(here, lanes - 1, 1), here),
        )
        beside = jnp.where(outer, 0.0, beside)
        field, lev = divmod(2 * v, levels)
        dynamic = gcm[at, :] + DT_DYN * (0.5 * (here + beside))
        out[at, :] = dynamic + jnp.where(low, feedback(field, lev), feedback(field, lev + 1))


def outer_kernel(hbm_inner, hbm_left, hbm_right, out, inner, left, right, sems):
    copies = fetch(((hbm_left, left), (hbm_right, right), (hbm_inner, inner)), sems)
    for copy in copies[:2]:
        copy.wait()
    rows, lanes = inner.shape
    width = left.shape[1]
    pair = jnp.concatenate([left[...], right[...], jnp.zeros((6, width), jnp.float32)], axis=0)
    row8, lane8 = rows_of((8, lanes)), lanes_of((8, lanes))
    spread = jnp.where((row8 < 2) & (lane8 == jnp.where(row8 == 0, 0, lanes - 1)), 1.0, 0.0)
    halo = split_dot(lax.dot_general, pair, spread, (((0,), (0,)), ((), ())))
    copies[2].wait()
    out[...] = inner[...] + (DT_DYN * 0.5) * halo[:rows]


def cloud_kernel(
    hbm_courant, hbm_relax, hbm_sat, hbm_cond, hbm_gcm, hbm_active, hbm_wind_x, hbm_wind_y, crm,
    new, hbm_change, hbm_tend,
    courant, relax, sat, cond_rate, gcm, active, wind_x, wind_y, change, tend,
    held, one, two, fixed, other, begin, profile, factors, sems, in_sem, out_sem, late_sem,
):
    copies = fetch(
        (
            (hbm_gcm, gcm),
            (hbm_relax, relax),
            (hbm_sat, sat),
            (hbm_courant, courant),
            (hbm_cond, cond_rate),
            (hbm_active, active),
            (hbm_wind_x, wind_x),
            (hbm_wind_y, wind_y),
        ),
        sems,
    )
    fields, levels, rows, lanes = crm.shape
    half_tiles = rows // 16
    tiles = rows // 8
    source_levels = profile.shape[1]
    middle = levels // 2
    cuts = [middle * c // PIECES for c in range(PIECES + 1)]
    pieces = [
        [
            (f, first, b - a)
            for first in (middle - b, middle + a)
            for f in range(fields)
        ]
        for a, b in zip(cuts[:-1], cuts[1:])
    ]
    low = rows_of((8, lanes)) < 4

    loads = [
        [
            pltpu.make_async_copy(
                crm.at[f, pl.ds(first, size)], held.at[f, pl.ds(first, size)], in_sem.at[c, i]
            )
            for i, (f, first, size) in enumerate(piece)
        ]
        for c, piece in enumerate(pieces)
    ]
    for group in loads:
        for load in group:
            load.start()
    for copy in copies:
        copy.wait()

    for f in range(fields):
        for v in range(source_levels // 2):
            base = (f * source_levels + 2 * v) * 4
            pair = gcm[base : base + 8, :].astype(jnp.bfloat16).astype(jnp.float32)
            swapped = pltpu.roll(pair, 4, 0)
            profile[f, 2 * v] = jnp.where(low, pair, swapped)
            profile[f, 2 * v + 1] = jnp.where(low, swapped, pair)
    for k, entries in enumerate(hat_rows(levels, source_levels)):
        for f in range(fields):
            total = None
            for l, weight in entries:
                term = weight * profile[f, l]
                total = term if total is None else total + term
            fixed[f, k] = total

    zero = jnp.zeros((8, lanes), jnp.float32)
    ratio, value = [zero] * (2 * fields), [zero] * (2 * fields)
    for i in range(middle):
        ends = KAPPA if i == 0 else 2.0 * KAPPA
        for f in range(fields):
            for side, k in enumerate((i, levels - 1 - i)):
                chain = 2 * f + side
                rate = DT_CLOUD * relax[f, k]
                scale = 1.0 / (
                    jnp.full((8, lanes), ends + rate, jnp.float32) - KAPPA * ratio[chain]
                )
                value[chain] = (rate * fixed[f, k] + KAPPA * value[chain]) * scale
                ratio[chain] = KAPPA * scale
                fixed[f, k] = value[chain]
                begin[f, k] = ratio[chain]
    carry = []
    for f in range(fields):
        (up_value, down_value), (up_ratio, down_ratio) = (x[2 * f : 2 * f + 2] for x in (value, ratio))
        below = (up_value + up_ratio * down_value) / (1.0 - up_ratio * down_ratio)
        carry += [down_value + down_ratio * below, below]
    tendency(source_levels, wind_x, wind_y, gcm, tend)
    late = [pltpu.make_async_copy(tend, hbm_tend, late_sem.at[0])]
    late[0].start()

    def unpack(i, carry):
        result = [None] * (2 * fields)
        for side, k in enumerate((middle - 1 - i, middle + i)):
            for f in range(fields):
                steady = fixed[f, k] + begin[f, k] * carry[2 * f + side]
                fixed[f, k] = steady
                result[2 * f + side] = steady
                block = held[f, k].astype(jnp.float32)
                total = zero
                for u in range(half_tiles):
                    near, far = (block[8 * t : 8 * t + 8] for t in (u, u + half_tiles))
                    even = jnp.where(low, near, pltpu.roll(far, 4, 0))
                    odd = jnp.where(low, pltpu.roll(near, 4, 0), far)
                    total = total + (even + odd)
                    one[f, k, 16 * u : 16 * u + 8, :] = even - steady
                    one[f, k, 16 * u + 8 : 16 * u + 16, :] = odd - steady
                begin[f, k] = total
            other[k] = result[2 + side] - sat[k]
        return tuple(result)

    carry = tuple(carry)
    for c in range(PIECES):
        for load in loads[c]:
            load.wait()
        carry = lax.fori_loop(cuts[c], cuts[c + 1], unpack, carry)

    for k in range(levels):
        for f in range(fields):
            keep = (1.0 - 2.0 * KAPPA - courant[k] - DT_CLOUD * relax[f, k]) * (1.0 / KAPPA)
            factors[f, k] = jnp.full((8, lanes), keep, jnp.float32)
        factors[fields, k] = jnp.full((8, lanes), courant[k] * (1.0 / KAPPA), jnp.float32)
        factors[fields + 1, k] = jnp.full((8, lanes), DT_CLOUD * cond_rate[k], jnp.float32)

    def substep(src, dst, scale, inverse):
        for k in range(levels):
            factors[fields + 2, k] = factors[fields + 1, k] * inverse

        def group(i, _):
            base = pl.multiple_of(i * 8 * GROUP, 8)
            beside = pl.multiple_of(lax.rem(base + rows - 8, rows), 8)
            turn = jnp.where(i == 0, 4, 0)

            def tiles_of(f, k):
                return [src[f, k, pl.ds(base + 8 * w, 8), :] for w in range(GROUP)]

            above = [tiles_of(f, 0) for f in range(fields)]
            here = above
            for k in range(levels):
                below = [tiles_of(f, min(k + 1, levels - 1)) for f in range(fields)]
                shift, rate, offset = factors[fields, k], factors[fields + 2, k], other[k]
                keep = [factors[f, k] for f in range(fields)]
                left = [
                    [pltpu.roll(src[f, k, pl.ds(beside, 8), :], turn, 0)] + here[f][:-1]
                    for f in range(fields)
                ]
                for w in range(GROUP):
                    condense = rate * jnp.tanh(here[1][w] * scale + offset)
                    for f in range(fields):
                        moved = (above[f][w] + below[f][w]) + (
                            keep[f] * here[f][w] + shift * left[f][w]
                        )
                        dst[f, k, pl.ds(base + 8 * w, 8), :] = (
                            moved + condense if f == 0 else moved - condense
                        )
                above, here = here, below
            return 0

        lax.fori_loop(0, tiles // GROUP, group, 0)

    def two_substeps(_, carry):
        scale, inverse = carry
        substep(one, two, scale, inverse)
        scale, inverse = scale * KAPPA, inverse * (1.0 / KAPPA)
        substep(two, one, scale, inverse)
        return scale * KAPPA, inverse * (1.0 / KAPPA)

    final, _ = lax.fori_loop(
        0, SUBSTEPS // 2, two_substeps, (jnp.float32(1.0), jnp.float32(1.0 / KAPPA))
    )

    chosen = jnp.concatenate([active[...], active[...]], axis=0) > 0
    chosen16 = jnp.concatenate([active[...]] * 4, axis=0).astype(jnp.bfloat16) > 0
    share = 4.0 / rows

    def pack(f):
        def at(k, _):
            steady = fixed[f, k]
            total = zero
            near, far = [], []
            for u in range(half_tiles):
                even = one[f, k, 16 * u : 16 * u + 8, :] * final + steady
                odd = one[f, k, 16 * u + 8 : 16 * u + 16, :] * final + steady
                total = total + (even + odd)
                near.append(jnp.where(low, even, pltpu.roll(odd, 4, 0)))
                far.append(jnp.where(low, pltpu.roll(even, 4, 0), odd))
            tiles_new = near + far
            for u in range(half_tiles):
                pair = jnp.concatenate(tiles_new[2 * u : 2 * u + 2], axis=0).astype(jnp.bfloat16)
                at16 = slice(16 * u, 16 * u + 16)
                held[f, k, at16, :] = jnp.where(chosen16, pair, held[f, k, at16, :])
            total = total - begin[f, k]
            total = (total + pltpu.roll(total, 4, 0)) * share
            total = total.astype(jnp.bfloat16).astype(jnp.float32)
            change[f, k] = jnp.where(chosen, total, 0.0)
            return 0

        return at

    for c in range(PIECES - 1, -1, -1):
        for i, (f, first, size) in enumerate(pieces[c]):
            lax.fori_loop(first, first + size, pack(f), 0, unroll=2)
            store = pltpu.make_async_copy(
                held.at[f, pl.ds(first, size)], new.at[f, pl.ds(first, size)], out_sem.at[c, i]
            )
            store.start()
            late.append(store)

    store = pltpu.make_async_copy(change, hbm_change, late_sem.at[1])
    store.start()
    late.append(store)
    for store in late:
        store.wait()


def body(gcm_state, crm_state, active, wind_x, wind_y, courant, relax, sat, cond_rate):
    fields, levels, rows_x, lanes = gcm_state.shape
    cloud_levels, cloud_columns = crm_state.shape[1:3]
    rows = fields * levels * rows_x
    gcm = gcm_state.reshape(rows, lanes)
    crm = crm_state.reshape(fields, cloud_levels, cloud_columns * rows_x, lanes)
    def kept(*arrays):
        return [pltpu.with_memory_space_constraint(a, pltpu.HBM) for a in arrays]

    vmem = pl.BlockSpec(memory_space=pltpu.VMEM)
    hbm = pl.BlockSpec(memory_space=pltpu.HBM)
    dma = pltpu.SemaphoreType.DMA
    f32 = jnp.float32
    width = (rows + 127) // 128 * 128

    def moved(cells, axis, step):
        size = lax.axis_size(axis)
        return lax.ppermute(cells, axis, [(i, (i + step) % size) for i in range(size)])

    before, after = moved(gcm, "col", 1), moved(gcm, "col", -1)

    slots = (fields, cloud_levels, cloud_columns * rows_x, lanes)
    tile = (fields, cloud_levels, 8, lanes)
    new, change, tend = pl.pallas_call(
        cloud_kernel,
        out_shape=(
            pltpu.HBM(slots, jnp.bfloat16),
            pltpu.HBM(tile, f32),
            pltpu.HBM((rows, lanes), f32),
        ),
        in_specs=[hbm] * 9,
        out_specs=(hbm,) * 3,
        scratch_shapes=[
            pltpu.SMEM(courant.shape, f32),
            pltpu.SMEM(relax.shape, f32),
            pltpu.SMEM(sat.shape, f32),
            pltpu.SMEM(cond_rate.shape, f32),
            pltpu.VMEM((rows, lanes), f32),
            pltpu.VMEM(active.shape, active.dtype),
            pltpu.SMEM(wind_x.shape, f32),
            pltpu.SMEM(wind_y.shape, f32),
            pltpu.VMEM(tile, f32),
            pltpu.VMEM((rows, lanes), f32),
            pltpu.VMEM(slots, jnp.bfloat16),
            pltpu.VMEM(slots, f32),
            pltpu.VMEM(slots, f32),
            pltpu.VMEM(tile, f32),
            pltpu.VMEM(tile[1:], f32),
            pltpu.VMEM(tile, f32),
            pltpu.VMEM((fields, levels, 8, lanes), f32),
            pltpu.VMEM((fields + 3, cloud_levels, 8, lanes), f32),
            dma((8,)),
            dma((PIECES, 2 * fields)),
            dma((PIECES, 2 * fields)),
            dma((2,)),
        ],
        compiler_params=pltpu.CompilerParams(vmem_limit_bytes=(64 << 20) - (256 << 10)),
        cost_estimate=pl.CostEstimate(
            flops=60_000_000, bytes_accessed=200_000_000, transcendentals=20_000_000
        ),
        name="cloud",
    )(*kept(courant, relax, sat, cond_rate, gcm, active, wind_x, wind_y, crm))

    shared, low_end, high_end = pl.pallas_call(
        functools.partial(share_kernel, levels),
        out_shape=(
            jax.ShapeDtypeStruct((rows, lanes), f32),
            jax.ShapeDtypeStruct((1, width), f32),
            jax.ShapeDtypeStruct((1, width), f32),
        ),
        in_specs=[hbm] * 5,
        out_specs=(vmem,) * 3,
        scratch_shapes=[
            pltpu.SMEM(wind_x.shape, f32),
            pltpu.SMEM(wind_y.shape, f32),
            pltpu.VMEM((rows, lanes), f32),
            pltpu.VMEM((rows, lanes), f32),
            pltpu.VMEM((rows, lanes), f32),
            pltpu.VMEM((rows, lanes), f32),
            pltpu.VMEM((2, levels * rows_x, lanes), f32),
            dma((5,)),
        ],
        name="share",
    )(*kept(wind_x, wind_y, before, after, tend))
    left, right = moved(high_end, "sub", 1), moved(low_end, "sub", -1)

    inner = pl.pallas_call(
        functools.partial(inner_kernel, levels, cloud_levels),
        out_shape=pltpu.HBM((rows, lanes), f32),
        in_specs=[hbm] * 3,
        out_specs=vmem,
        scratch_shapes=[
            pltpu.VMEM((rows, lanes), f32),
            pltpu.VMEM((rows, lanes), f32),
            pltpu.VMEM(tile, f32),
            dma((3,)),
        ],
        compiler_params=pltpu.CompilerParams(vmem_limit_bytes=64 << 20),
        cost_estimate=pl.CostEstimate(
            flops=1_000_000, bytes_accessed=5_000_000, transcendentals=0
        ),
        name="inner",
    )(*kept(gcm, shared, change))
    out = pl.pallas_call(
        outer_kernel,
        out_shape=jax.ShapeDtypeStruct((rows, lanes), f32),
        in_specs=[hbm] * 3,
        out_specs=vmem,
        scratch_shapes=[
            pltpu.VMEM((rows, lanes), f32),
            pltpu.VMEM((1, width), f32),
            pltpu.VMEM((1, width), f32),
            dma((3,)),
        ],
        name="outer",
    )(*kept(inner, left, right))
    return out.reshape(gcm_state.shape), new.reshape(crm_state.shape)


def solution(mesh):
    placed = (
        P(None, None, ("groups", "col"), "sub"),
        P(None, None, None, ("groups", "col"), "sub"),
        P(("groups", "col"), "sub"),
        P(),
        P(),
        P(),
        P(),
        P(),
        P(),
    )
    return jax.shard_map(
        body,
        mesh=mesh,
        in_specs=placed,
        out_specs=(
            P(None, None, ("groups", "col"), "sub"),
            P(None, None, None, ("groups", "col"), "sub"),
        ),
        check_vma=False,
    )
```

```python
import functools

import jax
import jax.numpy as jnp
import numpy as np
from jax import lax
from jax.experimental import pallas as pl
from jax.experimental.pallas import tpu as pltpu
from jax.sharding import PartitionSpec as P

SUBSTEPS = 24
DT_DYN = 0.05
DT_CLOUD = 0.5
KAPPA = 0.15
HIGH = lax.Precision.HIGHEST
GROUP = 4
PIECES = 1


def gll_derivative():
    nodes = np.array([-1.0, -1.0 / np.sqrt(5.0), 1.0 / np.sqrt(5.0), 1.0])
    weights = np.array(
        [1.0 / np.prod([nodes[j] - nodes[k] for k in range(4) if k != j]) for j in range(4)]
    )
    deriv = np.zeros((4, 4))
    for i in range(4):
        for j in range(4):
            if i != j:
                deriv[i, j] = weights[j] / weights[i] / (nodes[i] - nodes[j])
        deriv[i, i] = -deriv[i].sum()
    return 2.0 * deriv


def hat_rows(count_to, count_from):
    dest = (np.arange(count_to) + 0.5) / count_to
    source = (np.arange(count_from) + 0.5) / count_from
    hat = np.maximum(0.0, 1.0 - np.abs(dest[:, None] - source[None, :]) * count_from)
    hat = hat / hat.sum(axis=1, keepdims=True)
    return [[(int(c), float(row[c])) for c in np.nonzero(row > 1e-9)[0]] for row in hat]


def lanes_of(shape):
    return lax.broadcasted_iota(jnp.int32, shape, len(shape) - 1)


def rows_of(shape):
    return lax.broadcasted_iota(jnp.int32, shape, len(shape) - 2)


def fetch(pairs, sems):
    copies = [pltpu.make_async_copy(a, b, sems.at[i]) for i, (a, b) in enumerate(pairs)]
    for copy in copies:
        copy.start()
    return copies


def along_lanes(lanes):
    deriv = gll_derivative()
    side_a, side_b = rows_of((lanes, lanes)), lanes_of((lanes, lanes))
    step = jnp.zeros((lanes, lanes), jnp.float32)
    for m in range(4):
        for n in range(4):
            step = jnp.where((side_a % 4 == m) & (side_b % 4 == n), float(deriv[n, m]), step)
    return jnp.where(side_a // 4 == side_b // 4, step, 0.0)


def tendency(levels, wind_x, wind_y, gcm, tend):
    deriv = gll_derivative()
    rows, lanes = gcm.shape
    tend[...] = jnp.dot(
        gcm[...], along_lanes(lanes), precision=HIGH, preferred_element_type=jnp.float32
    )
    row = rows_of((8, lanes))
    low = row < 4
    factors = {}
    for shift in range(-3, 4):
        factor = jnp.zeros((8, lanes), jnp.float32)
        for i in range(4):
            if 0 <= i - shift < 4:
                factor = jnp.where(row % 4 == i, float(deriv[i, i - shift]), factor)
        factors[shift] = factor
    for v in range(rows // 8):
        at = slice(8 * v, 8 * v + 8)
        lev = 2 * v % levels
        here = gcm[at, :]
        along_x = factors[0] * here
        for shift in (-3, -2, -1, 1, 2, 3):
            along_x = along_x + factors[shift] * pltpu.roll(here, shift % 8, 0)
        blow_x = jnp.where(low, wind_x[lev], wind_x[lev + 1])
        blow_y = jnp.where(low, wind_y[lev], wind_y[lev + 1])
        tend[at, :] = -(blow_x * along_x + blow_y * tend[at, :])


def share_kernel(
    levels, hbm_wind_x, hbm_wind_y, hbm_before, hbm_after, hbm_tend, hbm_shared, hbm_end, hbm_other_end,
    wind_x, wind_y, near, tend, work, blow, end, other_end, sems, out_sems,
):
    copies = fetch(
        (
            (hbm_wind_x, wind_x),
            (hbm_wind_y, wind_y),
            (hbm_before, near.at[0]),
            (hbm_after, near.at[1]),
            (hbm_tend, tend),
        ),
        sems,
    )
    deriv = gll_derivative()
    rows, lanes = tend.shape
    fields = rows // (4 * levels)
    step = along_lanes(lanes)
    low = rows_of((8, lanes)) < 4
    for copy in copies[:2]:
        copy.wait()
    for v in range(levels // 2):
        at = slice(8 * v, 8 * v + 8)
        blow[0, at, :] = jnp.where(low, wind_x[2 * v], wind_x[2 * v + 1])
        blow[1, at, :] = jnp.where(low, wind_y[2 * v], wind_y[2 * v + 1])
    blow_x = blow[0, pl.ds(0, levels, stride=4), :]
    blow_y = blow[1, pl.ds(0, levels, stride=4), :]
    for copy in copies[2:]:
        copy.wait()
    odd = lax.axis_index("sub") % 2
    parts = [(f, side, node) for f in range(fields) for side, node in ((0, 3), (1, 0))]
    nodes = [
        [near[side, pl.ds(4 * levels * f + m, levels, stride=4), :] for m in range(4)]
        for f, side, _ in parts
    ]
    along_y = jnp.dot(
        jnp.concatenate([cells[node] for cells, (_, _, node) in zip(nodes, parts)], axis=0),
        step,
        precision=HIGH,
        preferred_element_type=jnp.float32,
    )
    work[...] = tend[...]
    for i, (f, _, node) in enumerate(parts):
        along_x = sum(float(deriv[node, m]) * nodes[i][m] for m in range(4))
        work[pl.ds(4 * levels * f + 3 - node, levels, stride=4), :] = -(
            blow_x * along_x + blow_y * along_y[levels * i : levels * (i + 1)]
        )
    lane8 = lanes_of((8, lanes))
    low_tile = high_tile = jnp.zeros((8, lanes), jnp.float32)
    for v in range(rows // 8):
        at = slice(8 * v, 8 * v + 8)
        here = 0.5 * (tend[at, :] + work[at, :])
        work[at, :] = here
        low_tile = jnp.where(lane8 == v, pltpu.roll(here, v, 1), low_tile)
        high_tile = jnp.where(lane8 == v, pltpu.roll(here, (v + 1) % lanes, 1), high_tile)
    end[...] = jnp.where(odd == 0, high_tile, low_tile)
    other_end[...] = jnp.where(odd == 0, low_tile, high_tile)
    for copy in fetch(
        ((end, hbm_end), (other_end, hbm_other_end), (work, hbm_shared)), out_sems
    ):
        copy.wait()


def inner_kernel(
    levels, cloud_levels, hbm_gcm, hbm_shared, hbm_change, out, gcm, shared, change, sems
):
    copies = fetch(((hbm_shared, shared), (hbm_gcm, gcm), (hbm_change, change)), sems)
    for copy in copies:
        copy.wait()
    rows, lanes = gcm.shape
    row8, lane8 = rows_of((8, lanes)), lanes_of((8, lanes))
    first, last = lane8 % 4 == 0, lane8 % 4 == 3
    outer = (lane8 == 0) | (lane8 == lanes - 1)
    low = row8 < 4
    hats = hat_rows(levels, cloud_levels)

    def feedback(field, lev):
        total = None
        for k, weight in hats[lev]:
            term = weight * change[field, k]
            total = term if total is None else total + term
        return total

    for v in range(rows // 8):
        at = slice(8 * v, 8 * v + 8)
        here = shared[at, :]
        beside = jnp.where(
            first,
            pltpu.roll(here, 1, 1),
            jnp.where(last, pltpu.roll(here, lanes - 1, 1), here),
        )
        beside = jnp.where(outer, 0.0, beside)
        field, lev = divmod(2 * v, levels)
        dynamic = gcm[at, :] + DT_DYN * (0.5 * (here + beside))
        out[at, :] = dynamic + jnp.where(low, feedback(field, lev), feedback(field, lev + 1))


def outer_kernel(
    hbm_inner, hbm_first, hbm_second, hbm_out, inner, met, sems, out_sem
):
    copies = fetch(
        ((hbm_first, met.at[0]), (hbm_second, met.at[1]), (hbm_inner, inner)), sems
    )
    for copy in copies:
        copy.wait()
    rows, lanes = inner.shape
    lane8 = lanes_of((8, lanes))
    odd = lax.axis_index("sub") % 2
    at_left, at_right = met[1 - odd] * (0.5 * DT_DYN), met[odd] * (0.5 * DT_DYN)
    for v in range(rows // 8):
        at = slice(8 * v, 8 * v + 8)
        halo = jnp.where(
            lane8 == 0,
            pltpu.roll(at_left, (lanes - v) % lanes, 1),
            jnp.where(lane8 == lanes - 1, pltpu.roll(at_right, lanes - 1 - v, 1), 0.0),
        )
        inner[at, :] = inner[at, :] + halo
    copy = pltpu.make_async_copy(inner, hbm_out, out_sem)
    copy.start()
    copy.wait()


def cloud_kernel(
    hbm_courant, hbm_relax, hbm_sat, hbm_cond, hbm_gcm, hbm_active, hbm_wind_x, hbm_wind_y, crm,
    new, hbm_change, hbm_tend,
    courant, relax, sat, cond_rate, gcm, active, wind_x, wind_y, change, tend,
    held, one, two, fixed, other, begin, profile, factors, sems, in_sem, out_sem, late_sem,
):
    copies = fetch(
        (
            (hbm_gcm, gcm),
            (hbm_relax, relax),
            (hbm_sat, sat),
            (hbm_courant, courant),
            (hbm_cond, cond_rate),
            (hbm_active, active),
            (hbm_wind_x, wind_x),
            (hbm_wind_y, wind_y),
        ),
        sems,
    )
    fields, levels, rows, lanes = crm.shape
    half_tiles = rows // 16
    tiles = rows // 8
    source_levels = profile.shape[1]
    middle = levels // 2
    cuts = [middle * c // PIECES for c in range(PIECES + 1)]
    pieces = [
        [
            (f, first, b - a)
            for first in (middle - b, middle + a)
            for f in range(fields)
        ]
        for a, b in zip(cuts[:-1], cuts[1:])
    ]
    low = rows_of((8, lanes)) < 4

    loads = [
        [
            pltpu.make_async_copy(
                crm.at[f, pl.ds(first, size)], held.at[f, pl.ds(first, size)], in_sem.at[c, i]
            )
            for i, (f, first, size) in enumerate(piece)
        ]
        for c, piece in enumerate(pieces)
    ]
    for group in loads:
        for load in group:
            load.start()
    for copy in copies:
        copy.wait()

    for f in range(fields):
        for v in range(source_levels // 2):
            base = (f * source_levels + 2 * v) * 4
            pair = gcm[base : base + 8, :].astype(jnp.bfloat16).astype(jnp.float32)
            swapped = pltpu.roll(pair, 4, 0)
            profile[f, 2 * v] = jnp.where(low, pair, swapped)
            profile[f, 2 * v + 1] = jnp.where(low, swapped, pair)
    for k, entries in enumerate(hat_rows(levels, source_levels)):
        for f in range(fields):
            total = None
            for l, weight in entries:
                term = weight * profile[f, l]
                total = term if total is None else total + term
            fixed[f, k] = total

    zero = jnp.zeros((8, lanes), jnp.float32)
    ratio, value = [zero] * (2 * fields), [zero] * (2 * fields)
    for i in range(middle):
        ends = KAPPA if i == 0 else 2.0 * KAPPA
        for f in range(fields):
            for side, k in enumerate((i, levels - 1 - i)):
                chain = 2 * f + side
                rate = DT_CLOUD * relax[f, k]
                scale = 1.0 / (
                    jnp.full((8, lanes), ends + rate, jnp.float32) - KAPPA * ratio[chain]
                )
                value[chain] = (rate * fixed[f, k] + KAPPA * value[chain]) * scale
                ratio[chain] = KAPPA * scale
                fixed[f, k] = value[chain]
                begin[f, k] = ratio[chain]
    carry = []
    for f in range(fields):
        (up_value, down_value), (up_ratio, down_ratio) = (x[2 * f : 2 * f + 2] for x in (value, ratio))
        below = (up_value + up_ratio * down_value) / (1.0 - up_ratio * down_ratio)
        carry += [down_value + down_ratio * below, below]
    tendency(source_levels, wind_x, wind_y, gcm, tend)
    late = [pltpu.make_async_copy(tend, hbm_tend, late_sem.at[0])]
    late[0].start()

    def unpack(i, carry):
        result = [None] * (2 * fields)
        for side, k in enumerate((middle - 1 - i, middle + i)):
            for f in range(fields):
                steady = fixed[f, k] + begin[f, k] * carry[2 * f + side]
                fixed[f, k] = steady
                result[2 * f + side] = steady
                block = held[f, k].astype(jnp.float32)
                total = zero
                for u in range(half_tiles):
                    near, far = (block[8 * t : 8 * t + 8] for t in (u, u + half_tiles))
                    even = jnp.where(low, near, pltpu.roll(far, 4, 0))
                    odd = jnp.where(low, pltpu.roll(near, 4, 0), far)
                    total = total + (even + odd)
                    one[f, k, 16 * u : 16 * u + 8, :] = even - steady
                    one[f, k, 16 * u + 8 : 16 * u + 16, :] = odd - steady
                begin[f, k] = total
            other[k] = result[2 + side] - sat[k]
        return tuple(result)

    carry = tuple(carry)
    for c in range(PIECES):
        for load in loads[c]:
            load.wait()
        carry = lax.fori_loop(cuts[c], cuts[c + 1], unpack, carry, unroll=2)

    for k in range(levels):
        for f in range(fields):
            keep = (1.0 - 2.0 * KAPPA - courant[k] - DT_CLOUD * relax[f, k]) * (1.0 / KAPPA)
            factors[f, k] = jnp.full((8, lanes), keep, jnp.float32)
        factors[fields, k] = jnp.full((8, lanes), courant[k] * (1.0 / KAPPA), jnp.float32)
        factors[fields + 1, k] = jnp.full((8, lanes), DT_CLOUD * cond_rate[k], jnp.float32)

    def substep(src, dst, scale, inverse):
        for k in range(levels):
            factors[fields + 2, k] = factors[fields + 1, k] * inverse

        def group(i, _):
            base = pl.multiple_of(i * 8 * GROUP, 8)
            beside = pl.multiple_of(lax.rem(base + rows - 8, rows), 8)
            turn = jnp.where(i == 0, 4, 0)

            def tiles_of(f, k):
                return [src[f, k, pl.ds(base + 8 * w, 8), :] for w in range(GROUP)]

            above = [tiles_of(f, 0) for f in range(fields)]
            here = above
            for k in range(levels):
                below = [tiles_of(f, min(k + 1, levels - 1)) for f in range(fields)]
                shift, rate, offset = factors[fields, k], factors[fields + 2, k], other[k]
                keep = [factors[f, k] for f in range(fields)]
                left = [
                    [pltpu.roll(src[f, k, pl.ds(beside, 8), :], turn, 0)] + here[f][:-1]
                    for f in range(fields)
                ]
                for w in range(GROUP):
                    condense = rate * jnp.tanh(here[1][w] * scale + offset)
                    for f in range(fields):
                        moved = (above[f][w] + below[f][w]) + (
                            keep[f] * here[f][w] + shift * left[f][w]
                        )
                        dst[f, k, pl.ds(base + 8 * w, 8), :] = (
                            moved + condense if f == 0 else moved - condense
                        )
                above, here = here, below
            return 0

        lax.fori_loop(0, tiles // GROUP, group, 0)

    def two_substeps(_, carry):
        scale, inverse = carry
        substep(one, two, scale, inverse)
        scale, inverse = scale * KAPPA, inverse * (1.0 / KAPPA)
        substep(two, one, scale, inverse)
        return scale * KAPPA, inverse * (1.0 / KAPPA)

    final, _ = lax.fori_loop(
        0, SUBSTEPS // 2, two_substeps, (jnp.float32(1.0), jnp.float32(1.0 / KAPPA))
    )

    chosen = jnp.concatenate([active[...], active[...]], axis=0) > 0
    chosen16 = jnp.concatenate([active[...]] * 4, axis=0).astype(jnp.bfloat16) > 0
    share = 4.0 / rows

    def pack(f):
        def at(k, _):
            steady = fixed[f, k]
            total = zero
            near, far = [], []
            for u in range(half_tiles):
                even = one[f, k, 16 * u : 16 * u + 8, :] * final + steady
                odd = one[f, k, 16 * u + 8 : 16 * u + 16, :] * final + steady
                total = total + (even + odd)
                near.append(jnp.where(low, even, pltpu.roll(odd, 4, 0)))
                far.append(jnp.where(low, pltpu.roll(even, 4, 0), odd))
            tiles_new = near + far
            for u in range(half_tiles):
                pair = jnp.concatenate(tiles_new[2 * u : 2 * u + 2], axis=0).astype(jnp.bfloat16)
                at16 = slice(16 * u, 16 * u + 16)
                held[f, k, at16, :] = jnp.where(chosen16, pair, held[f, k, at16, :])
            total = total - begin[f, k]
            total = (total + pltpu.roll(total, 4, 0)) * share
            total = total.astype(jnp.bfloat16).astype(jnp.float32)
            change[f, k] = jnp.where(chosen, total, 0.0)
            return 0

        return at

    for c in range(PIECES - 1, -1, -1):
        for i, (f, first, size) in enumerate(pieces[c]):
            lax.fori_loop(first, first + size, pack(f), 0, unroll=4)
            store = pltpu.make_async_copy(
                held.at[f, pl.ds(first, size)], new.at[f, pl.ds(first, size)], out_sem.at[c, i]
            )
            store.start()
            late.append(store)

    store = pltpu.make_async_copy(change, hbm_change, late_sem.at[1])
    store.start()
    late.append(store)
    for store in late:
        store.wait()


def body(gcm_state, crm_state, active, wind_x, wind_y, courant, relax, sat, cond_rate):
    fields, levels, rows_x, lanes = gcm_state.shape
    cloud_levels, cloud_columns = crm_state.shape[1:3]
    rows = fields * levels * rows_x
    gcm = gcm_state.reshape(rows, lanes)
    crm = crm_state.reshape(fields, cloud_levels, cloud_columns * rows_x, lanes)
    def kept(*arrays):
        return [pltpu.with_memory_space_constraint(a, pltpu.HBM) for a in arrays]

    vmem = pl.BlockSpec(memory_space=pltpu.VMEM)
    hbm = pl.BlockSpec(memory_space=pltpu.HBM)
    dma = pltpu.SemaphoreType.DMA
    f32 = jnp.float32

    def swapped(cells, axis, first):
        size = lax.axis_size(axis)
        pairs = [((i + first) % size, (i + 1 + first) % size) for i in range(0, size, 2)]
        return lax.ppermute(cells, axis, pairs + [(b, a) for a, b in pairs])

    size_x = lax.axis_size("col")
    ring = [(i, (i + 1) % size_x) for i in range(size_x)]
    beside = lax.ppermute(gcm, "col", ring), lax.ppermute(gcm, "col", [(b, a) for a, b in ring])

    slots = (fields, cloud_levels, cloud_columns * rows_x, lanes)
    tile = (fields, cloud_levels, 8, lanes)
    new, change, tend = pl.pallas_call(
        cloud_kernel,
        out_shape=(
            pltpu.HBM(slots, jnp.bfloat16),
            pltpu.HBM(tile, f32),
            pltpu.HBM((rows, lanes), f32),
        ),
        in_specs=[hbm] * 9,
        out_specs=(hbm,) * 3,
        scratch_shapes=[
            pltpu.SMEM(courant.shape, f32),
            pltpu.SMEM(relax.shape, f32),
            pltpu.SMEM(sat.shape, f32),
            pltpu.SMEM(cond_rate.shape, f32),
            pltpu.VMEM((rows, lanes), f32),
            pltpu.VMEM(active.shape, active.dtype),
            pltpu.SMEM(wind_x.shape, f32),
            pltpu.SMEM(wind_y.shape, f32),
            pltpu.VMEM(tile, f32),
            pltpu.VMEM((rows, lanes), f32),
            pltpu.VMEM(slots, jnp.bfloat16),
            pltpu.VMEM(slots, f32),
            pltpu.VMEM(slots, f32),
            pltpu.VMEM(tile, f32),
            pltpu.VMEM(tile[1:], f32),
            pltpu.VMEM(tile, f32),
            pltpu.VMEM((fields, levels, 8, lanes), f32),
            pltpu.VMEM((fields + 3, cloud_levels, 8, lanes), f32),
            dma((8,)),
            dma((PIECES, 2 * fields)),
            dma((PIECES, 2 * fields)),
            dma((2,)),
        ],
        compiler_params=pltpu.CompilerParams(vmem_limit_bytes=(64 << 20) - (256 << 10)),
        cost_estimate=pl.CostEstimate(
            flops=60_000_000, bytes_accessed=200_000_000, transcendentals=20_000_000
        ),
        name="cloud",
    )(*kept(courant, relax, sat, cond_rate, gcm, active, wind_x, wind_y, crm))

    shared, *ends = pl.pallas_call(
        functools.partial(share_kernel, levels),
        out_shape=(
            pltpu.HBM((rows, lanes), f32),
            pltpu.HBM((8, lanes), f32),
            pltpu.HBM((8, lanes), f32),
        ),
        in_specs=[hbm] * 5,
        out_specs=(hbm,) * 3,
        scratch_shapes=[
            pltpu.SMEM(wind_x.shape, f32),
            pltpu.SMEM(wind_y.shape, f32),
            pltpu.VMEM((2, rows, lanes), f32),
            pltpu.VMEM((rows, lanes), f32),
            pltpu.VMEM((rows, lanes), f32),
            pltpu.VMEM((2, levels * rows_x, lanes), f32),
            pltpu.VMEM((8, lanes), f32),
            pltpu.VMEM((8, lanes), f32),
            dma((5,)),
            dma((3,)),
        ],
        name="share",
    )(*kept(wind_x, wind_y, *beside, tend))
    met = swapped(ends[0], "sub", 0), swapped(ends[1], "sub", 1)

    inner = pl.pallas_call(
        functools.partial(inner_kernel, levels, cloud_levels),
        out_shape=pltpu.HBM((rows, lanes), f32),
        in_specs=[hbm] * 3,
        out_specs=vmem,
        scratch_shapes=[
            pltpu.VMEM((rows, lanes), f32),
            pltpu.VMEM((rows, lanes), f32),
            pltpu.VMEM(tile, f32),
            dma((3,)),
        ],
        compiler_params=pltpu.CompilerParams(vmem_limit_bytes=64 << 20),
        cost_estimate=pl.CostEstimate(
            flops=1_000_000, bytes_accessed=5_000_000, transcendentals=0
        ),
        name="inner",
    )(*kept(gcm, shared, change))
    out = pl.pallas_call(
        outer_kernel,
        out_shape=pltpu.HBM((rows, lanes), f32),
        in_specs=[hbm] * 3,
        out_specs=hbm,
        scratch_shapes=[
            pltpu.VMEM((rows, lanes), f32),
            pltpu.VMEM((2, 8, lanes), f32),
            dma((3,)),
            dma,
        ],
        name="outer",
    )(*kept(inner, *met))
    return out.reshape(gcm_state.shape), new.reshape(crm_state.shape)


def solution(mesh):
    placed = (
        P(None, None, ("groups", "col"), "sub"),
        P(None, None, None, ("groups", "col"), "sub"),
        P(("groups", "col"), "sub"),
        P(),
        P(),
        P(),
        P(),
        P(),
        P(),
    )
    return jax.shard_map(
        body,
        mesh=mesh,
        in_specs=placed,
        out_specs=(
            P(None, None, ("groups", "col"), "sub"),
            P(None, None, None, ("groups", "col"), "sub"),
        ),
        check_vma=False,
    )
```

```python
import functools

import jax
import jax.numpy as jnp
import numpy as np
from jax import lax
from jax.experimental import pallas as pl
from jax.experimental.pallas import tpu as pltpu
from jax.sharding import PartitionSpec as P

SUBSTEPS = 24
DT_DYN = 0.05
DT_CLOUD = 0.5
KAPPA = 0.15
HIGH = lax.Precision.HIGHEST
GROUP = 4
PIECES = 1


def gll_derivative():
    nodes = np.array([-1.0, -1.0 / np.sqrt(5.0), 1.0 / np.sqrt(5.0), 1.0])
    weights = np.array(
        [1.0 / np.prod([nodes[j] - nodes[k] for k in range(4) if k != j]) for j in range(4)]
    )
    deriv = np.zeros((4, 4))
    for i in range(4):
        for j in range(4):
            if i != j:
                deriv[i, j] = weights[j] / weights[i] / (nodes[i] - nodes[j])
        deriv[i, i] = -deriv[i].sum()
    return 2.0 * deriv


def hat_rows(count_to, count_from):
    dest = (np.arange(count_to) + 0.5) / count_to
    source = (np.arange(count_from) + 0.5) / count_from
    hat = np.maximum(0.0, 1.0 - np.abs(dest[:, None] - source[None, :]) * count_from)
    hat = hat / hat.sum(axis=1, keepdims=True)
    return [[(int(c), float(row[c])) for c in np.nonzero(row > 1e-9)[0]] for row in hat]


def lanes_of(shape):
    return lax.broadcasted_iota(jnp.int32, shape, len(shape) - 1)


def rows_of(shape):
    return lax.broadcasted_iota(jnp.int32, shape, len(shape) - 2)


def fetch(pairs, sems):
    copies = [pltpu.make_async_copy(a, b, sems.at[i]) for i, (a, b) in enumerate(pairs)]
    for copy in copies:
        copy.start()
    return copies


def along_lanes(lanes):
    deriv = gll_derivative()
    side_a, side_b = rows_of((lanes, lanes)), lanes_of((lanes, lanes))
    step = jnp.zeros((lanes, lanes), jnp.float32)
    for m in range(4):
        for n in range(4):
            step = jnp.where((side_a % 4 == m) & (side_b % 4 == n), float(deriv[n, m]), step)
    return jnp.where(side_a // 4 == side_b // 4, step, 0.0)


def tendency(levels, wind_x, wind_y, gcm, tend):
    deriv = gll_derivative()
    rows, lanes = gcm.shape
    tend[...] = jnp.dot(
        gcm[...], along_lanes(lanes), precision=HIGH, preferred_element_type=jnp.float32
    )
    row = rows_of((8, lanes))
    low = row < 4
    factors = {}
    for shift in range(-3, 4):
        factor = jnp.zeros((8, lanes), jnp.float32)
        for i in range(4):
            if 0 <= i - shift < 4:
                factor = jnp.where(row % 4 == i, float(deriv[i, i - shift]), factor)
        factors[shift] = factor
    for v in range(rows // 8):
        at = slice(8 * v, 8 * v + 8)
        lev = 2 * v % levels
        here = gcm[at, :]
        along_x = factors[0] * here
        for shift in (-3, -2, -1, 1, 2, 3):
            along_x = along_x + factors[shift] * pltpu.roll(here, shift % 8, 0)
        blow_x = jnp.where(low, wind_x[lev], wind_x[lev + 1])
        blow_y = jnp.where(low, wind_y[lev], wind_y[lev + 1])
        tend[at, :] = -(blow_x * along_x + blow_y * tend[at, :])


def share_kernel(
    levels, hbm_wind_x, hbm_wind_y, hbm_before, hbm_after, hbm_tend, hbm_shared, hbm_end, hbm_other_end,
    wind_x, wind_y, near, tend, work, blow, end, other_end, sems, out_sems,
):
    rows, lanes = tend.shape
    copies = fetch(
        (
            (hbm_wind_x, wind_x),
            (hbm_wind_y, wind_y),
            (hbm_before, near.at[0, pl.ds(0, rows)]),
            (hbm_after, near.at[1, pl.ds(0, rows)]),
            (hbm_tend, tend),
        ),
        sems,
    )
    deriv = gll_derivative()
    fields = rows // (4 * levels)
    step = along_lanes(lanes)
    low = rows_of((8, lanes)) < 4
    for copy in copies[:2]:
        copy.wait()
    for v in range(levels // 2):
        at = slice(8 * v, 8 * v + 8)
        blow[0, at, :] = jnp.where(low, wind_x[2 * v], wind_x[2 * v + 1])
        blow[1, at, :] = jnp.where(low, wind_y[2 * v], wind_y[2 * v + 1])
    blow_x = blow[0, pl.ds(0, levels, stride=4), :]
    blow_y = blow[1, pl.ds(0, levels, stride=4), :]
    for copy in copies[2:]:
        copy.wait()
    odd = lax.axis_index("sub") % 2
    parts = [(f, side, node) for f in range(fields) for side, node in ((0, 3), (1, 0))]
    nodes = [
        [near[side, pl.ds(4 * levels * f + m, levels, stride=4), :] for m in range(4)]
        for f, side, _ in parts
    ]
    along_y = jnp.dot(
        jnp.concatenate([cells[node] for cells, (_, _, node) in zip(nodes, parts)], axis=0),
        step,
        precision=HIGH,
        preferred_element_type=jnp.float32,
    )
    work[:rows, :] = tend[...]
    for i, (f, _, node) in enumerate(parts):
        along_x = sum(float(deriv[node, m]) * nodes[i][m] for m in range(4))
        work[pl.ds(4 * levels * f + 3 - node, levels, stride=4), :] = -(
            blow_x * along_x + blow_y * along_y[levels * i : levels * (i + 1)]
        )
    lane8 = lanes_of((8, lanes))
    low_tile = high_tile = jnp.zeros((8, lanes), jnp.float32)
    for v in range(rows // 8):
        at = slice(8 * v, 8 * v + 8)
        here = 0.5 * (tend[at, :] + work[at, :])
        work[at, :] = here
        low_tile = jnp.where(lane8 == v, pltpu.roll(here, v, 1), low_tile)
        high_tile = jnp.where(lane8 == v, pltpu.roll(here, (v + 1) % lanes, 1), high_tile)
    end[...] = jnp.where(odd == 0, high_tile, low_tile)
    other_end[...] = jnp.where(odd == 0, low_tile, high_tile)
    for copy in fetch(
        ((end, hbm_end), (other_end, hbm_other_end), (work.at[pl.ds(0, rows)], hbm_shared)), out_sems
    ):
        copy.wait()


def inner_kernel(
    levels, cloud_levels, hbm_gcm, hbm_shared, hbm_change, out, gcm, shared, change, sems
):
    copies = fetch(((hbm_shared, shared), (hbm_gcm, gcm), (hbm_change, change)), sems)
    for copy in copies:
        copy.wait()
    rows, lanes = gcm.shape
    row8, lane8 = rows_of((8, lanes)), lanes_of((8, lanes))
    first, last = lane8 % 4 == 0, lane8 % 4 == 3
    outer = (lane8 == 0) | (lane8 == lanes - 1)
    low = row8 < 4
    hats = hat_rows(levels, cloud_levels)

    def feedback(field, lev):
        total = None
        for k, weight in hats[lev]:
            term = weight * change[field, k]
            total = term if total is None else total + term
        return total

    for v in range(rows // 8):
        at = slice(8 * v, 8 * v + 8)
        here = shared[at, :]
        beside = jnp.where(
            first,
            pltpu.roll(here, 1, 1),
            jnp.where(last, pltpu.roll(here, lanes - 1, 1), here),
        )
        beside = jnp.where(outer, 0.0, beside)
        field, lev = divmod(2 * v, levels)
        dynamic = gcm[at, :] + DT_DYN * (0.5 * (here + beside))
        out[at, :] = dynamic + jnp.where(low, feedback(field, lev), feedback(field, lev + 1))


def outer_kernel(
    hbm_inner, hbm_first, hbm_second, hbm_out, inner, met, sems, out_sem
):
    copies = fetch(
        ((hbm_first, met.at[0]), (hbm_second, met.at[1]), (hbm_inner, inner)), sems
    )
    for copy in copies:
        copy.wait()
    rows, lanes = inner.shape
    lane8 = lanes_of((8, lanes))
    odd = lax.axis_index("sub") % 2
    at_left, at_right = met[1 - odd] * (0.5 * DT_DYN), met[odd] * (0.5 * DT_DYN)
    for v in range(rows // 8):
        at = slice(8 * v, 8 * v + 8)
        halo = jnp.where(
            lane8 == 0,
            pltpu.roll(at_left, (lanes - v) % lanes, 1),
            jnp.where(lane8 == lanes - 1, pltpu.roll(at_right, lanes - 1 - v, 1), 0.0),
        )
        inner[at, :] = inner[at, :] + halo
    copy = pltpu.make_async_copy(inner, hbm_out, out_sem)
    copy.start()
    copy.wait()


def cloud_kernel(
    hbm_courant, hbm_relax, hbm_sat, hbm_cond, hbm_gcm, hbm_active, hbm_wind_x, hbm_wind_y, crm,
    new, hbm_change, hbm_tend,
    courant, relax, sat, cond_rate, gcm, active, wind_x, wind_y, change, tend,
    held, one, two, fixed, other, begin, profile, factors, sems, in_sem, out_sem, late_sem,
):
    copies = fetch(
        (
            (hbm_gcm, gcm),
            (hbm_relax, relax),
            (hbm_sat, sat),
            (hbm_courant, courant),
            (hbm_cond, cond_rate),
            (hbm_active, active),
            (hbm_wind_x, wind_x),
            (hbm_wind_y, wind_y),
        ),
        sems,
    )
    fields, levels, rows, lanes = crm.shape
    half_tiles = rows // 16
    tiles = rows // 8
    source_levels = profile.shape[1]
    middle = levels // 2
    cuts = [middle * c // PIECES for c in range(PIECES + 1)]
    pieces = [
        [
            (f, first, b - a)
            for first in (middle - b, middle + a)
            for f in range(fields)
        ]
        for a, b in zip(cuts[:-1], cuts[1:])
    ]
    low = rows_of((8, lanes)) < 4

    loads = [
        [
            pltpu.make_async_copy(
                crm.at[f, pl.ds(first, size)], held.at[f, pl.ds(first, size)], in_sem.at[c, i]
            )
            for i, (f, first, size) in enumerate(piece)
        ]
        for c, piece in enumerate(pieces)
    ]
    for group in loads:
        for load in group:
            load.start()
    for copy in copies:
        copy.wait()

    for f in range(fields):
        for v in range(source_levels // 2):
            base = (f * source_levels + 2 * v) * 4
            pair = gcm[base : base + 8, :].astype(jnp.bfloat16).astype(jnp.float32)
            swapped = pltpu.roll(pair, 4, 0)
            profile[f, 2 * v] = jnp.where(low, pair, swapped)
            profile[f, 2 * v + 1] = jnp.where(low, swapped, pair)
    for k, entries in enumerate(hat_rows(levels, source_levels)):
        for f in range(fields):
            total = None
            for l, weight in entries:
                term = weight * profile[f, l]
                total = term if total is None else total + term
            fixed[f, k] = total

    zero = jnp.zeros((8, lanes), jnp.float32)
    ratio, value = [zero] * (2 * fields), [zero] * (2 * fields)
    for i in range(middle):
        ends = KAPPA if i == 0 else 2.0 * KAPPA
        for f in range(fields):
            for side, k in enumerate((i, levels - 1 - i)):
                chain = 2 * f + side
                rate = DT_CLOUD * relax[f, k]
                scale = 1.0 / (
                    jnp.full((8, lanes), ends + rate, jnp.float32) - KAPPA * ratio[chain]
                )
                value[chain] = (rate * fixed[f, k] + KAPPA * value[chain]) * scale
                ratio[chain] = KAPPA * scale
                fixed[f, k] = value[chain]
                begin[f, k] = ratio[chain]
    carry = []
    for f in range(fields):
        (up_value, down_value), (up_ratio, down_ratio) = (x[2 * f : 2 * f + 2] for x in (value, ratio))
        below = (up_value + up_ratio * down_value) / (1.0 - up_ratio * down_ratio)
        carry += [down_value + down_ratio * below, below]
    tendency(source_levels, wind_x, wind_y, gcm, tend)
    late = [pltpu.make_async_copy(tend, hbm_tend, late_sem.at[0])]
    late[0].start()

    least = KAPPA**SUBSTEPS

    def unpack(i, carry):
        result = [None] * (2 * fields)
        for side, k in enumerate((middle - 1 - i, middle + i)):
            for f in range(fields):
                steady = fixed[f, k] + begin[f, k] * carry[2 * f + side]
                fixed[f, k] = steady
                result[2 * f + side] = steady
                block = held[f, k].astype(jnp.float32)
                total = zero
                for u in range(half_tiles):
                    near, far = (block[8 * t : 8 * t + 8] for t in (u, u + half_tiles))
                    even = jnp.where(low, near, pltpu.roll(far, 4, 0))
                    odd = jnp.where(low, pltpu.roll(near, 4, 0), far)
                    total = total + (even + odd)
                    one[f, k, 16 * u : 16 * u + 8, :] = (even - steady) * least
                    one[f, k, 16 * u + 8 : 16 * u + 16, :] = (odd - steady) * least
                begin[f, k] = total
            other[k] = result[2 + side] - sat[k]
        return tuple(result)

    carry = tuple(carry)
    for c in range(PIECES):
        for load in loads[c]:
            load.wait()
        carry = lax.fori_loop(cuts[c], cuts[c + 1], unpack, carry, unroll=4)

    for k in range(levels):
        for f in range(fields):
            keep = (1.0 - 2.0 * KAPPA - courant[k] - DT_CLOUD * relax[f, k]) * (1.0 / KAPPA)
            factors[f, k] = jnp.full((8, lanes), keep, jnp.float32)
        factors[fields, k] = jnp.full((8, lanes), courant[k] * (1.0 / KAPPA), jnp.float32)
        factors[fields + 1, k] = jnp.full((8, lanes), DT_CLOUD * cond_rate[k], jnp.float32)

    def substep(src, dst, scale, inverse):
        for k in range(levels):
            factors[fields + 2, k] = factors[fields + 1, k] * inverse

        def group(i, _):
            base = pl.multiple_of(i * 8 * GROUP, 8)
            beside = pl.multiple_of(lax.rem(base + rows - 8, rows), 8)
            turn = jnp.where(i == 0, 4, 0)

            def tiles_of(f, k):
                return [src[f, k, pl.ds(base + 8 * w, 8), :] for w in range(GROUP)]

            above = [tiles_of(f, 0) for f in range(fields)]
            here = above
            for k in range(levels):
                below = [tiles_of(f, min(k + 1, levels - 1)) for f in range(fields)]
                shift, rate, offset = factors[fields, k], factors[fields + 2, k], other[k]
                keep = [factors[f, k] for f in range(fields)]
                left = [
                    [pltpu.roll(src[f, k, pl.ds(beside, 8), :], turn, 0)] + here[f][:-1]
                    for f in range(fields)
                ]
                for w in range(GROUP):
                    condense = rate * jnp.tanh(here[1][w] * scale + offset)
                    for f in range(fields):
                        moved = (above[f][w] + below[f][w]) + (
                            keep[f] * here[f][w] + shift * left[f][w]
                        )
                        dst[f, k, pl.ds(base + 8 * w, 8), :] = (
                            moved + condense if f == 0 else moved - condense
                        )
                above, here = here, below
            return 0

        lax.fori_loop(0, tiles // GROUP, group, 0)

    def two_substeps(_, carry):
        scale, inverse = carry
        substep(one, two, scale, inverse)
        scale, inverse = scale * KAPPA, inverse * (1.0 / KAPPA)
        substep(two, one, scale, inverse)
        return scale * KAPPA, inverse * (1.0 / KAPPA)

    lax.fori_loop(
        0, SUBSTEPS // 2, two_substeps, (jnp.float32(1.0 / least), jnp.float32(least / KAPPA))
    )

    chosen = jnp.concatenate([active[...], active[...]], axis=0) > 0
    chosen16 = jnp.concatenate([active[...]] * 4, axis=0).astype(jnp.bfloat16) > 0
    share = 4.0 / rows

    def pack(f):
        def at(k, _):
            steady = fixed[f, k]
            total = zero
            near, far = [], []
            for u in range(half_tiles):
                even = one[f, k, 16 * u : 16 * u + 8, :] + steady
                odd = one[f, k, 16 * u + 8 : 16 * u + 16, :] + steady
                total = total + (even + odd)
                near.append(jnp.where(low, even, pltpu.roll(odd, 4, 0)))
                far.append(jnp.where(low, pltpu.roll(even, 4, 0), odd))
            tiles_new = near + far
            for u in range(half_tiles):
                pair = jnp.concatenate(tiles_new[2 * u : 2 * u + 2], axis=0).astype(jnp.bfloat16)
                at16 = slice(16 * u, 16 * u + 16)
                held[f, k, at16, :] = jnp.where(chosen16, pair, held[f, k, at16, :])
            total = total - begin[f, k]
            total = (total + pltpu.roll(total, 4, 0)) * share
            total = total.astype(jnp.bfloat16).astype(jnp.float32)
            change[f, k] = jnp.where(chosen, total, 0.0)
            return 0

        return at

    for c in range(PIECES - 1, -1, -1):
        for i, (f, first, size) in enumerate(pieces[c]):
            lax.fori_loop(first, first + size, pack(f), 0, unroll=4)
            store = pltpu.make_async_copy(
                held.at[f, pl.ds(first, size)], new.at[f, pl.ds(first, size)], out_sem.at[c, i]
            )
            store.start()
            late.append(store)

    store = pltpu.make_async_copy(change, hbm_change, late_sem.at[1])
    store.start()
    late.append(store)
    for store in late:
        store.wait()


def body(gcm_state, crm_state, active, wind_x, wind_y, courant, relax, sat, cond_rate):
    fields, levels, rows_x, lanes = gcm_state.shape
    cloud_levels, cloud_columns = crm_state.shape[1:3]
    rows = fields * levels * rows_x
    gcm = gcm_state.reshape(rows, lanes)
    crm = crm_state.reshape(fields, cloud_levels, cloud_columns * rows_x, lanes)
    def kept(*arrays):
        return [pltpu.with_memory_space_constraint(a, pltpu.HBM) for a in arrays]

    vmem = pl.BlockSpec(memory_space=pltpu.VMEM)
    hbm = pl.BlockSpec(memory_space=pltpu.HBM)
    dma = pltpu.SemaphoreType.DMA
    f32 = jnp.float32

    def swapped(cells, axis, first):
        size = lax.axis_size(axis)
        pairs = [((i + first) % size, (i + 1 + first) % size) for i in range(0, size, 2)]
        return lax.ppermute(cells, axis, pairs + [(b, a) for a, b in pairs])

    size_x = lax.axis_size("col")
    ring = [(i, (i + 1) % size_x) for i in range(size_x)]
    beside = lax.ppermute(gcm, "col", ring), lax.ppermute(gcm, "col", [(b, a) for a, b in ring])

    slots = (fields, cloud_levels, cloud_columns * rows_x, lanes)
    tile = (fields, cloud_levels, 8, lanes)
    new, change, tend = pl.pallas_call(
        cloud_kernel,
        out_shape=(
            pltpu.HBM(slots, jnp.bfloat16),
            pltpu.HBM(tile, f32),
            pltpu.HBM((rows, lanes), f32),
        ),
        in_specs=[hbm] * 9,
        out_specs=(hbm,) * 3,
        scratch_shapes=[
            pltpu.SMEM(courant.shape, f32),
            pltpu.SMEM(relax.shape, f32),
            pltpu.SMEM(sat.shape, f32),
            pltpu.SMEM(cond_rate.shape, f32),
            pltpu.VMEM((rows, lanes), f32),
            pltpu.VMEM(active.shape, active.dtype),
            pltpu.SMEM(wind_x.shape, f32),
            pltpu.SMEM(wind_y.shape, f32),
            pltpu.VMEM(tile, f32),
            pltpu.VMEM((rows, lanes), f32),
            pltpu.VMEM(slots, jnp.bfloat16),
            pltpu.VMEM(slots, f32),
            pltpu.VMEM(slots, f32),
            pltpu.VMEM(tile, f32),
            pltpu.VMEM(tile[1:], f32),
            pltpu.VMEM(tile, f32),
            pltpu.VMEM((fields, levels, 8, lanes), f32),
            pltpu.VMEM((fields + 3, cloud_levels, 8, lanes), f32),
            dma((8,)),
            dma((PIECES, 2 * fields)),
            dma((PIECES, 2 * fields)),
            dma((2,)),
        ],
        compiler_params=pltpu.CompilerParams(vmem_limit_bytes=(64 << 20) - (256 << 10)),
        cost_estimate=pl.CostEstimate(
            flops=60_000_000, bytes_accessed=200_000_000, transcendentals=20_000_000
        ),
        name="cloud",
    )(*kept(courant, relax, sat, cond_rate, gcm, active, wind_x, wind_y, crm))

    shared, *ends = pl.pallas_call(
        functools.partial(share_kernel, levels),
        out_shape=(
            pltpu.HBM((rows, lanes), f32),
            pltpu.HBM((8, lanes), f32),
            pltpu.HBM((8, lanes), f32),
        ),
        in_specs=[hbm] * 5,
        out_specs=(hbm,) * 3,
        scratch_shapes=[
            pltpu.SMEM(wind_x.shape, f32),
            pltpu.SMEM(wind_y.shape, f32),
            pltpu.VMEM((2, rows + 8, lanes), f32),
            pltpu.VMEM((rows, lanes), f32),
            pltpu.VMEM((rows + 8, lanes), f32),
            pltpu.VMEM((2, levels * rows_x + 8, lanes), f32),
            pltpu.VMEM((8, lanes), f32),
            pltpu.VMEM((8, lanes), f32),
            dma((5,)),
            dma((3,)),
        ],
        name="share",
    )(*kept(wind_x, wind_y, *beside, tend))
    met = swapped(ends[0], "sub", 0), swapped(ends[1], "sub", 1)

    inner = pl.pallas_call(
        functools.partial(inner_kernel, levels, cloud_levels),
        out_shape=pltpu.HBM((rows, lanes), f32),
        in_specs=[hbm] * 3,
        out_specs=vmem,
        scratch_shapes=[
            pltpu.VMEM((rows, lanes), f32),
            pltpu.VMEM((rows, lanes), f32),
            pltpu.VMEM(tile, f32),
            dma((3,)),
        ],
        compiler_params=pltpu.CompilerParams(vmem_limit_bytes=64 << 20),
        cost_estimate=pl.CostEstimate(
            flops=1_000_000, bytes_accessed=5_000_000, transcendentals=0
        ),
        name="inner",
    )(*kept(gcm, shared, change))
    out = pl.pallas_call(
        outer_kernel,
        out_shape=pltpu.HBM((rows, lanes), f32),
        in_specs=[hbm] * 3,
        out_specs=hbm,
        scratch_shapes=[
            pltpu.VMEM((rows, lanes), f32),
            pltpu.VMEM((2, 8, lanes), f32),
            dma((3,)),
            dma,
        ],
        name="outer",
    )(*kept(inner, *met))
    return out.reshape(gcm_state.shape), new.reshape(crm_state.shape)


def solution(mesh):
    placed = (
        P(None, None, ("groups", "col"), "sub"),
        P(None, None, None, ("groups", "col"), "sub"),
        P(("groups", "col"), "sub"),
        P(),
        P(),
        P(),
        P(),
        P(),
        P(),
    )
    return jax.shard_map(
        body,
        mesh=mesh,
        in_specs=placed,
        out_specs=(
            P(None, None, ("groups", "col"), "sub"),
            P(None, None, None, ("groups", "col"), "sub"),
        ),
        check_vma=False,
    )
```

```python
import functools

import jax
import jax.numpy as jnp
import numpy as np
from jax import lax
from jax.experimental import pallas as pl
from jax.experimental.pallas import tpu as pltpu
from jax.sharding import PartitionSpec as P

SUBSTEPS = 24
DT_DYN = 0.05
DT_CLOUD = 0.5
KAPPA = 0.15
HIGH = lax.Precision.HIGHEST
GROUP = 4
PIECES = 1


def gll_derivative():
    nodes = np.array([-1.0, -1.0 / np.sqrt(5.0), 1.0 / np.sqrt(5.0), 1.0])
    weights = np.array(
        [1.0 / np.prod([nodes[j] - nodes[k] for k in range(4) if k != j]) for j in range(4)]
    )
    deriv = np.zeros((4, 4))
    for i in range(4):
        for j in range(4):
            if i != j:
                deriv[i, j] = weights[j] / weights[i] / (nodes[i] - nodes[j])
        deriv[i, i] = -deriv[i].sum()
    return 2.0 * deriv


def hat_rows(count_to, count_from):
    dest = (np.arange(count_to) + 0.5) / count_to
    source = (np.arange(count_from) + 0.5) / count_from
    hat = np.maximum(0.0, 1.0 - np.abs(dest[:, None] - source[None, :]) * count_from)
    hat = hat / hat.sum(axis=1, keepdims=True)
    return [[(int(c), float(row[c])) for c in np.nonzero(row > 1e-9)[0]] for row in hat]


def lanes_of(shape):
    return lax.broadcasted_iota(jnp.int32, shape, len(shape) - 1)


def rows_of(shape):
    return lax.broadcasted_iota(jnp.int32, shape, len(shape) - 2)


def fetch(pairs, sems):
    copies = [pltpu.make_async_copy(a, b, sems.at[i]) for i, (a, b) in enumerate(pairs)]
    for copy in copies:
        copy.start()
    return copies


def along_lanes(lanes):
    deriv = gll_derivative()
    side_a, side_b = rows_of((lanes, lanes)), lanes_of((lanes, lanes))
    step = jnp.zeros((lanes, lanes), jnp.float32)
    for m in range(4):
        for n in range(4):
            step = jnp.where((side_a % 4 == m) & (side_b % 4 == n), float(deriv[n, m]), step)
    return jnp.where(side_a // 4 == side_b // 4, step, 0.0)


def tendency(levels, wind_x, wind_y, gcm, tend):
    deriv = gll_derivative()
    rows, lanes = gcm.shape
    tend[...] = jnp.dot(
        gcm[...], along_lanes(lanes), precision=HIGH, preferred_element_type=jnp.float32
    )
    row = rows_of((8, lanes))
    low = row < 4
    factors = {}
    for shift in range(-3, 4):
        factor = jnp.zeros((8, lanes), jnp.float32)
        for i in range(4):
            if 0 <= i - shift < 4:
                factor = jnp.where(row % 4 == i, float(deriv[i, i - shift]), factor)
        factors[shift] = factor
    for v in range(rows // 8):
        at = slice(8 * v, 8 * v + 8)
        lev = 2 * v % levels
        here = gcm[at, :]
        along_x = factors[0] * here
        for shift in (-3, -2, -1, 1, 2, 3):
            along_x = along_x + factors[shift] * pltpu.roll(here, shift % 8, 0)
        blow_x = jnp.where(low, wind_x[lev], wind_x[lev + 1])
        blow_y = jnp.where(low, wind_y[lev], wind_y[lev + 1])
        tend[at, :] = -(blow_x * along_x + blow_y * tend[at, :])


def share_kernel(
    levels, hbm_wind_x, hbm_wind_y, hbm_before, hbm_after, hbm_tend, hbm_shared, hbm_end, hbm_other_end,
    wind_x, wind_y, near, tend, work, blow, end, other_end, sems, out_sems,
):
    rows, lanes = tend.shape
    copies = fetch(
        (
            (hbm_wind_x, wind_x),
            (hbm_wind_y, wind_y),
            (hbm_before, near.at[0, pl.ds(0, rows)]),
            (hbm_after, near.at[1, pl.ds(0, rows)]),
            (hbm_tend, tend),
        ),
        sems,
    )
    deriv = gll_derivative()
    fields = rows // (4 * levels)
    step = along_lanes(lanes)
    low = rows_of((8, lanes)) < 4
    for copy in copies[:2]:
        copy.wait()
    for v in range(levels // 2):
        at = slice(8 * v, 8 * v + 8)
        blow[0, at, :] = jnp.where(low, wind_x[2 * v], wind_x[2 * v + 1])
        blow[1, at, :] = jnp.where(low, wind_y[2 * v], wind_y[2 * v + 1])
    blow_x = blow[0, pl.ds(0, levels, stride=4), :]
    blow_y = blow[1, pl.ds(0, levels, stride=4), :]
    for copy in copies[2:]:
        copy.wait()
    odd = lax.axis_index("sub") % 2
    parts = [(f, side, node) for f in range(fields) for side, node in ((0, 3), (1, 0))]
    nodes = [
        [near[side, pl.ds(4 * levels * f + m, levels, stride=4), :] for m in range(4)]
        for f, side, _ in parts
    ]
    along_y = jnp.dot(
        jnp.concatenate([cells[node] for cells, (_, _, node) in zip(nodes, parts)], axis=0),
        step,
        precision=HIGH,
        preferred_element_type=jnp.float32,
    )
    work[:rows, :] = tend[...]
    for i, (f, _, node) in enumerate(parts):
        along_x = sum(float(deriv[node, m]) * nodes[i][m] for m in range(4))
        work[pl.ds(4 * levels * f + 3 - node, levels, stride=4), :] = -(
            blow_x * along_x + blow_y * along_y[levels * i : levels * (i + 1)]
        )
    lane8 = lanes_of((8, lanes))
    low_tile = high_tile = jnp.zeros((8, lanes), jnp.float32)
    for v in range(rows // 8):
        at = slice(8 * v, 8 * v + 8)
        here = 0.5 * (tend[at, :] + work[at, :])
        work[at, :] = here
        low_tile = jnp.where(lane8 == v, pltpu.roll(here, v, 1), low_tile)
        high_tile = jnp.where(lane8 == v, pltpu.roll(here, (v + 1) % lanes, 1), high_tile)
    end[...] = jnp.where(odd == 0, high_tile, low_tile)
    other_end[...] = jnp.where(odd == 0, low_tile, high_tile)
    for copy in fetch(
        ((end, hbm_end), (other_end, hbm_other_end), (work.at[pl.ds(0, rows)], hbm_shared)), out_sems
    ):
        copy.wait()


def inner_kernel(
    levels, cloud_levels, hbm_gcm, hbm_shared, hbm_change, out, gcm, shared, change, sems
):
    copies = fetch(((hbm_shared, shared), (hbm_gcm, gcm), (hbm_change, change)), sems)
    for copy in copies:
        copy.wait()
    rows, lanes = gcm.shape
    row8, lane8 = rows_of((8, lanes)), lanes_of((8, lanes))
    first, last = lane8 % 4 == 0, lane8 % 4 == 3
    outer = (lane8 == 0) | (lane8 == lanes - 1)
    low = row8 < 4
    hats = hat_rows(levels, cloud_levels)

    def feedback(field, lev):
        total = None
        for k, weight in hats[lev]:
            term = weight * change[field, k]
            total = term if total is None else total + term
        return total

    for v in range(rows // 8):
        at = slice(8 * v, 8 * v + 8)
        here = shared[at, :]
        beside = jnp.where(
            first,
            pltpu.roll(here, 1, 1),
            jnp.where(last, pltpu.roll(here, lanes - 1, 1), here),
        )
        beside = jnp.where(outer, 0.0, beside)
        field, lev = divmod(2 * v, levels)
        dynamic = gcm[at, :] + DT_DYN * (0.5 * (here + beside))
        out[at, :] = dynamic + jnp.where(low, feedback(field, lev), feedback(field, lev + 1))


def outer_kernel(
    hbm_inner, hbm_first, hbm_second, hbm_out, inner, met, halo, sems, out_sem
):
    copies = fetch(
        ((hbm_first, met.at[0]), (hbm_second, met.at[1]), (hbm_inner, inner)), sems
    )
    for copy in copies[:2]:
        copy.wait()
    rows, lanes = inner.shape
    lane8 = lanes_of((8, lanes))
    odd = lax.axis_index("sub") % 2
    at_left, at_right = met[1 - odd] * (0.5 * DT_DYN), met[odd] * (0.5 * DT_DYN)
    for v in range(rows // 8):
        at = slice(8 * v, 8 * v + 8)
        halo[at, :] = jnp.where(
            lane8 == 0,
            pltpu.roll(at_left, (lanes - v) % lanes, 1),
            jnp.where(lane8 == lanes - 1, pltpu.roll(at_right, lanes - 1 - v, 1), 0.0),
        )
    copies[2].wait()
    inner[...] = inner[...] + halo[...]
    copy = pltpu.make_async_copy(inner, hbm_out, out_sem)
    copy.start()
    copy.wait()


def cloud_kernel(
    hbm_courant, hbm_relax, hbm_sat, hbm_cond, hbm_gcm, hbm_active, hbm_wind_x, hbm_wind_y, crm,
    new, hbm_change, hbm_tend,
    courant, relax, sat, cond_rate, gcm, active, wind_x, wind_y, change, tend,
    held, one, two, fixed, other, begin, profile, factors, sems, in_sem, out_sem, late_sem,
):
    copies = fetch(
        (
            (hbm_gcm, gcm),
            (hbm_relax, relax),
            (hbm_sat, sat),
            (hbm_courant, courant),
            (hbm_cond, cond_rate),
            (hbm_active, active),
            (hbm_wind_x, wind_x),
            (hbm_wind_y, wind_y),
        ),
        sems,
    )
    fields, levels, rows, lanes = crm.shape
    half_tiles = rows // 16
    tiles = rows // 8
    source_levels = profile.shape[1]
    middle = levels // 2
    cuts = [middle * c // PIECES for c in range(PIECES + 1)]
    pieces = [
        [
            (f, first, b - a)
            for first in (middle - b, middle + a)
            for f in range(fields)
        ]
        for a, b in zip(cuts[:-1], cuts[1:])
    ]
    low = rows_of((8, lanes)) < 4

    loads = [
        [
            pltpu.make_async_copy(
                crm.at[f, pl.ds(first, size)], held.at[f, pl.ds(first, size)], in_sem.at[c, i]
            )
            for i, (f, first, size) in enumerate(piece)
        ]
        for c, piece in enumerate(pieces)
    ]
    for group in loads:
        for load in group:
            load.start()
    for copy in copies:
        copy.wait()

    for f in range(fields):
        for v in range(source_levels // 2):
            base = (f * source_levels + 2 * v) * 4
            pair = gcm[base : base + 8, :].astype(jnp.bfloat16).astype(jnp.float32)
            swapped = pltpu.roll(pair, 4, 0)
            profile[f, 2 * v] = jnp.where(low, pair, swapped)
            profile[f, 2 * v + 1] = jnp.where(low, swapped, pair)
    for k, entries in enumerate(hat_rows(levels, source_levels)):
        for f in range(fields):
            total = None
            for l, weight in entries:
                term = weight * profile[f, l]
                total = term if total is None else total + term
            fixed[f, k] = total

    zero = jnp.zeros((8, lanes), jnp.float32)
    ratio, value = [zero] * (2 * fields), [zero] * (2 * fields)
    for i in range(middle):
        ends = KAPPA if i == 0 else 2.0 * KAPPA
        for f in range(fields):
            for side, k in enumerate((i, levels - 1 - i)):
                chain = 2 * f + side
                rate = DT_CLOUD * relax[f, k]
                scale = 1.0 / (
                    jnp.full((8, lanes), ends + rate, jnp.float32) - KAPPA * ratio[chain]
                )
                value[chain] = (rate * fixed[f, k] + KAPPA * value[chain]) * scale
                ratio[chain] = KAPPA * scale
                fixed[f, k] = value[chain]
                begin[f, k] = ratio[chain]
    carry = []
    for f in range(fields):
        (up_value, down_value), (up_ratio, down_ratio) = (x[2 * f : 2 * f + 2] for x in (value, ratio))
        below = (up_value + up_ratio * down_value) / (1.0 - up_ratio * down_ratio)
        carry += [down_value + down_ratio * below, below]
    tendency(source_levels, wind_x, wind_y, gcm, tend)
    late = [pltpu.make_async_copy(tend, hbm_tend, late_sem.at[0])]
    late[0].start()

    least = KAPPA**SUBSTEPS

    def unpack(i, carry):
        result = [None] * (2 * fields)
        for side, k in enumerate((middle - 1 - i, middle + i)):
            for f in range(fields):
                steady = fixed[f, k] + begin[f, k] * carry[2 * f + side]
                fixed[f, k] = steady
                result[2 * f + side] = steady
                block = held[f, k].astype(jnp.float32)
                total = zero
                for u in range(half_tiles):
                    near, far = (block[8 * t : 8 * t + 8] for t in (u, u + half_tiles))
                    even = jnp.where(low, near, pltpu.roll(far, 4, 0))
                    odd = jnp.where(low, pltpu.roll(near, 4, 0), far)
                    total = total + (even + odd)
                    one[f, k, 16 * u : 16 * u + 8, :] = (even - steady) * least
                    one[f, k, 16 * u + 8 : 16 * u + 16, :] = (odd - steady) * least
                begin[f, k] = total
            other[k] = result[2 + side] - sat[k]
        return tuple(result)

    for k in range(levels):
        for f in range(fields):
            keep = (1.0 - 2.0 * KAPPA - courant[k] - DT_CLOUD * relax[f, k]) * (1.0 / KAPPA)
            factors[f, k] = jnp.full((8, lanes), keep, jnp.float32)
        factors[fields, k] = jnp.full((8, lanes), courant[k] * (1.0 / KAPPA), jnp.float32)
        factors[fields + 1, k] = jnp.full((8, lanes), DT_CLOUD * cond_rate[k], jnp.float32)

    carry = tuple(carry)
    for c in range(PIECES):
        for load in loads[c]:
            load.wait()
        carry = lax.fori_loop(cuts[c], cuts[c + 1], unpack, carry, unroll=4)

    def substep(src, dst, scale, inverse):
        for k in range(levels):
            factors[fields + 2, k] = factors[fields + 1, k] * inverse

        def group(i, _):
            base = pl.multiple_of(i * 8 * GROUP, 8)
            beside = pl.multiple_of(lax.rem(base + rows - 8, rows), 8)
            turn = jnp.where(i == 0, 4, 0)

            def tiles_of(f, k):
                return [src[f, k, pl.ds(base + 8 * w, 8), :] for w in range(GROUP)]

            above = [tiles_of(f, 0) for f in range(fields)]
            here = above
            for k in range(levels):
                below = [tiles_of(f, min(k + 1, levels - 1)) for f in range(fields)]
                shift, rate, offset = factors[fields, k], factors[fields + 2, k], other[k]
                keep = [factors[f, k] for f in range(fields)]
                left = [
                    [pltpu.roll(src[f, k, pl.ds(beside, 8), :], turn, 0)] + here[f][:-1]
                    for f in range(fields)
                ]
                for w in range(GROUP):
                    condense = rate * jnp.tanh(here[1][w] * scale + offset)
                    for f in range(fields):
                        moved = (above[f][w] + below[f][w]) + (
                            keep[f] * here[f][w] + shift * left[f][w]
                        )
                        dst[f, k, pl.ds(base + 8 * w, 8), :] = (
                            moved + condense if f == 0 else moved - condense
                        )
                above, here = here, below
            return 0

        lax.fori_loop(0, tiles // GROUP, group, 0)

    def two_substeps(_, carry):
        scale, inverse = carry
        substep(one, two, scale, inverse)
        scale, inverse = scale * KAPPA, inverse * (1.0 / KAPPA)
        substep(two, one, scale, inverse)
        return scale * KAPPA, inverse * (1.0 / KAPPA)

    lax.fori_loop(
        0, SUBSTEPS // 2, two_substeps, (jnp.float32(1.0 / least), jnp.float32(least / KAPPA))
    )

    chosen = jnp.concatenate([active[...], active[...]], axis=0) > 0
    chosen16 = jnp.concatenate([active[...]] * 4, axis=0).astype(jnp.bfloat16) > 0
    share = 4.0 / rows

    def pack(f):
        def at(k, _):
            steady = fixed[f, k]
            total = zero
            near, far = [], []
            for u in range(half_tiles):
                even = one[f, k, 16 * u : 16 * u + 8, :] + steady
                odd = one[f, k, 16 * u + 8 : 16 * u + 16, :] + steady
                total = total + (even + odd)
                near.append(jnp.where(low, even, pltpu.roll(odd, 4, 0)))
                far.append(jnp.where(low, pltpu.roll(even, 4, 0), odd))
            tiles_new = near + far
            for u in range(half_tiles):
                pair = jnp.concatenate(tiles_new[2 * u : 2 * u + 2], axis=0).astype(jnp.bfloat16)
                at16 = slice(16 * u, 16 * u + 16)
                held[f, k, at16, :] = jnp.where(chosen16, pair, held[f, k, at16, :])
            total = total - begin[f, k]
            total = (total + pltpu.roll(total, 4, 0)) * share
            total = total.astype(jnp.bfloat16).astype(jnp.float32)
            change[f, k] = jnp.where(chosen, total, 0.0)
            return 0

        return at

    for c in range(PIECES - 1, -1, -1):
        for i, (f, first, size) in enumerate(pieces[c]):
            lax.fori_loop(first, first + size, pack(f), 0, unroll=4)
            store = pltpu.make_async_copy(
                held.at[f, pl.ds(first, size)], new.at[f, pl.ds(first, size)], out_sem.at[c, i]
            )
            store.start()
            late.append(store)

    store = pltpu.make_async_copy(change, hbm_change, late_sem.at[1])
    store.start()
    late.append(store)
    for store in late:
        store.wait()


def body(gcm_state, crm_state, active, wind_x, wind_y, courant, relax, sat, cond_rate):
    fields, levels, rows_x, lanes = gcm_state.shape
    cloud_levels, cloud_columns = crm_state.shape[1:3]
    rows = fields * levels * rows_x
    gcm = gcm_state.reshape(rows, lanes)
    crm = crm_state.reshape(fields, cloud_levels, cloud_columns * rows_x, lanes)
    def kept(*arrays):
        return [pltpu.with_memory_space_constraint(a, pltpu.HBM) for a in arrays]

    vmem = pl.BlockSpec(memory_space=pltpu.VMEM)
    hbm = pl.BlockSpec(memory_space=pltpu.HBM)
    dma = pltpu.SemaphoreType.DMA
    f32 = jnp.float32

    def swapped(cells, axis, first):
        size = lax.axis_size(axis)
        pairs = [((i + first) % size, (i + 1 + first) % size) for i in range(0, size, 2)]
        return lax.ppermute(cells, axis, pairs + [(b, a) for a, b in pairs])

    size_x = lax.axis_size("col")
    ring = [(i, (i + 1) % size_x) for i in range(size_x)]
    beside = lax.ppermute(gcm, "col", ring), lax.ppermute(gcm, "col", [(b, a) for a, b in ring])

    slots = (fields, cloud_levels, cloud_columns * rows_x, lanes)
    tile = (fields, cloud_levels, 8, lanes)
    new, change, tend = pl.pallas_call(
        cloud_kernel,
        out_shape=(
            pltpu.HBM(slots, jnp.bfloat16),
            pltpu.HBM(tile, f32),
            pltpu.HBM((rows, lanes), f32),
        ),
        in_specs=[hbm] * 9,
        out_specs=(hbm,) * 3,
        scratch_shapes=[
            pltpu.SMEM(courant.shape, f32),
            pltpu.SMEM(relax.shape, f32),
            pltpu.SMEM(sat.shape, f32),
            pltpu.SMEM(cond_rate.shape, f32),
            pltpu.VMEM((rows, lanes), f32),
            pltpu.VMEM(active.shape, active.dtype),
            pltpu.SMEM(wind_x.shape, f32),
            pltpu.SMEM(wind_y.shape, f32),
            pltpu.VMEM(tile, f32),
            pltpu.VMEM((rows, lanes), f32),
            pltpu.VMEM(slots, jnp.bfloat16),
            pltpu.VMEM(slots, f32),
            pltpu.VMEM(slots, f32),
            pltpu.VMEM(tile, f32),
            pltpu.VMEM(tile[1:], f32),
            pltpu.VMEM(tile, f32),
            pltpu.VMEM((fields, levels, 8, lanes), f32),
            pltpu.VMEM((fields + 3, cloud_levels, 8, lanes), f32),
            dma((8,)),
            dma((PIECES, 2 * fields)),
            dma((PIECES, 2 * fields)),
            dma((2,)),
        ],
        compiler_params=pltpu.CompilerParams(vmem_limit_bytes=(64 << 20) - (256 << 10)),
        cost_estimate=pl.CostEstimate(
            flops=60_000_000, bytes_accessed=200_000_000, transcendentals=20_000_000
        ),
        name="cloud",
    )(*kept(courant, relax, sat, cond_rate, gcm, active, wind_x, wind_y, crm))

    shared, *ends = pl.pallas_call(
        functools.partial(share_kernel, levels),
        out_shape=(
            pltpu.HBM((rows, lanes), f32),
            pltpu.HBM((8, lanes), f32),
            pltpu.HBM((8, lanes), f32),
        ),
        in_specs=[hbm] * 5,
        out_specs=(hbm,) * 3,
        scratch_shapes=[
            pltpu.SMEM(wind_x.shape, f32),
            pltpu.SMEM(wind_y.shape, f32),
            pltpu.VMEM((2, rows + 8, lanes), f32),
            pltpu.VMEM((rows, lanes), f32),
            pltpu.VMEM((rows + 8, lanes), f32),
            pltpu.VMEM((2, levels * rows_x + 8, lanes), f32),
            pltpu.VMEM((8, lanes), f32),
            pltpu.VMEM((8, lanes), f32),
            dma((5,)),
            dma((3,)),
        ],
        name="share",
    )(*kept(wind_x, wind_y, *beside, tend))
    met = swapped(ends[0], "sub", 0), swapped(ends[1], "sub", 1)

    inner = pl.pallas_call(
        functools.partial(inner_kernel, levels, cloud_levels),
        out_shape=pltpu.HBM((rows, lanes), f32),
        in_specs=[hbm] * 3,
        out_specs=vmem,
        scratch_shapes=[
            pltpu.VMEM((rows, lanes), f32),
            pltpu.VMEM((rows, lanes), f32),
            pltpu.VMEM(tile, f32),
            dma((3,)),
        ],
        compiler_params=pltpu.CompilerParams(vmem_limit_bytes=64 << 20),
        cost_estimate=pl.CostEstimate(
            flops=1_000_000, bytes_accessed=5_000_000, transcendentals=0
        ),
        name="inner",
    )(*kept(gcm, shared, change))
    out = pl.pallas_call(
        outer_kernel,
        out_shape=pltpu.HBM((rows, lanes), f32),
        in_specs=[hbm] * 3,
        out_specs=hbm,
        scratch_shapes=[
            pltpu.VMEM((rows, lanes), f32),
            pltpu.VMEM((2, 8, lanes), f32),
            pltpu.VMEM((rows, lanes), f32),
            dma((3,)),
            dma,
        ],
        name="outer",
    )(*kept(inner, *met))
    return out.reshape(gcm_state.shape), new.reshape(crm_state.shape)


def solution(mesh):
    placed = (
        P(None, None, ("groups", "col"), "sub"),
        P(None, None, None, ("groups", "col"), "sub"),
        P(("groups", "col"), "sub"),
        P(),
        P(),
        P(),
        P(),
        P(),
        P(),
    )
    return jax.shard_map(
        body,
        mesh=mesh,
        in_specs=placed,
        out_specs=(
            P(None, None, ("groups", "col"), "sub"),
            P(None, None, None, ("groups", "col"), "sub"),
        ),
        check_vma=False,
    )
```
